256 devices in a mesh: dp: 4 (over x_lo, core), seq: 64 (over x_hi, z, y).
Axes of the slice: x: 4 (x_hi: 2, x_lo: 2; x = x_hi * 2 + x_lo), y: 4, z: 8, core: 2. Of those that a mesh axis runs over, the one named last changes fastest.
Arguments:
- tokens: bfloat16 [4, 64, 256, 1152], P('dp', 'seq'), parts along dimension 0, may hold values from -6 to 6
- w_qkv: bfloat16 [2, 1152, 3456], P(None, None, 'seq'), may hold values from -1 to 1
- w_out: bfloat16 [2, 1152, 1152], P(None, None, 'seq'), may hold values from -0.1875 to 0.1875
- mod_shift: float32 [2, 1152], replicated, may hold values from -3 to 3
- mod_scale: float32 [2, 1152], replicated, may hold values from 0.5 to 2
- mod_gate: float32 [2, 1152], replicated, may hold values from 0.5 to 1.5
Outputs:
- result: bfloat16 [4, 64, 256, 1152], P('dp', 'seq'), parts along dimension 0
The draws below stay inside these ranges and needn't reach their ends.
There are 4 independent parts, one for each index of `dp`. The reference program is written for one: setup_inputs(seed, part) draws one part's arguments, and reference() takes and returns one part's arrays. A program takes and returns all parts, laid end to end along the dimension named above; an argument that names none is the same for every part. Nothing has to cross between parts.
All inputs are finite; a program needn't handle non-finite values.
Results may differ from the reference program's by a relative error of at most 0.017.
Values may be sent and summed in bfloat16 or wider, within the bound.
A program may use at most 128 MiB of HBM per device.

```python
import math
import jax
import jax.numpy as jnp
from jax import lax

D = 1152
HEADS = 16
HEAD_DIM = 72
PATCHES = 256
CLIPS = 1
FRAMES = 64


def draw_w_qkv(key, part):
    key = jax.random.fold_in(key, 5)
    first = jax.random.fold_in(key, 0)
    base = jnp.clip(jax.random.normal(first, (2, D, 3 * D), jnp.float32), -6.0, 6.0) / math.sqrt(D)
    return base.astype(jnp.bfloat16)


def levels(key, extent, cuts, smallest, largest):
    factor_of = 1.0
    for position, blocks in cuts:
        heights = jax.random.uniform(jax.random.fold_in(jax.random.fold_in(key, 6), position), (blocks,), jnp.float32, smallest / len(cuts), largest / len(cuts))
        factor_of = factor_of * jnp.repeat(jnp.exp(heights), extent[position] // blocks).reshape((-1,) + (1,) * (len(extent) - 1 - position))
    return factor_of


def normal_values(stream_key, shape, scale, bound, shards=(), held_as=jnp.bfloat16):
    drawn = jax.random.normal(stream_key, shape, jnp.float32) * scale
    if len(shards) > 0:
        drawn = levels(stream_key, shape, shards, -0.22, 0.18) * drawn
    return jnp.clip(drawn, min=-bound, max=bound).astype(held_as)


def setup_inputs(seed: int = 0, part: int = 0) -> dict:
    key_of = jax.random.split(jax.random.key(seed), 7)
    part_splits = jax.random.split(jax.random.fold_in(key_of[6], part), 7)
    tokens = normal_values(part_splits[0], (CLIPS, FRAMES, PATCHES, D), 1.0, 6.0, ((1, 64),))
    w_qkv = draw_w_qkv(jax.random.fold_in(key_of[6], 71), part)
    w_out = normal_values(key_of[2], (2, D, D), D ** -0.5, 0.1875, ((2, 64),))
    mod_shift = normal_values(key_of[3], (2, D), 0.5, 3.0, (), jnp.float32)
    mod_scale = jnp.clip(jnp.exp(jax.random.uniform(key_of[4], (2, D), jnp.float32, math.log(0.5), math.log(2.0))), 0.5, 2.0)
    mod_gate = jnp.clip(jax.random.uniform(key_of[5], (2, D), jnp.float32, 0.5, 1.5), 0.5, 1.5)
    return {"tokens": tokens, "w_qkv": w_qkv, "w_out": w_out, "mod_shift": mod_shift, "mod_scale": mod_scale, "mod_gate": mod_gate}


def modulate(rows, shift, scale):
    values = rows.astype(jnp.float32)
    mean = lax.optimization_barrier(jnp.mean(values, axis=-1, keepdims=True))
    centred = values - mean
    spread = lax.optimization_barrier(jnp.mean(centred * centred, axis=-1, keepdims=True))
    return (centred * lax.rsqrt(spread + 1e-06) * scale + shift).astype(jnp.bfloat16)

def attend(packed):
    batch, length, triple = packed.shape
    width = triple // 3
    query = packed[:, :, :width].reshape(batch, length, HEADS, HEAD_DIM).astype(jnp.float32)
    keys = packed[:, :, width:2 * width].reshape(batch, length, HEADS, HEAD_DIM).astype(jnp.float32)
    values = packed[:, :, 2 * width:].reshape(batch, length, HEADS, HEAD_DIM).astype(jnp.float32)
    scores = jnp.einsum('blhd,bmhd->bhlm', query, keys) * HEAD_DIM ** (-0.5)
    scores = scores - lax.optimization_barrier(jnp.max(scores, axis=-1, keepdims=True))
    weights = jnp.exp(scores)
    weights = (weights / lax.optimization_barrier(jnp.sum(weights, axis=-1, keepdims=True))).astype(jnp.bfloat16)
    mixed = jnp.einsum('bhlm,bmhd->blhd', weights.astype(jnp.float32), values)
    return mixed.astype(jnp.bfloat16).reshape(batch, length, width)

def one_clip(tokens, w_qkv, w_out, mod_shift, mod_scale, mod_gate):
    frames, patches, width = tokens.shape
    flat = tokens.reshape(frames * patches, width)
    normed_a = modulate(flat, mod_shift[0], mod_scale[0])
    qkv_a = jnp.dot(normed_a, w_qkv[0], preferred_element_type=jnp.float32).astype(jnp.bfloat16)
    qkv_a = qkv_a.reshape(frames, patches, 3 * width)
    spatial = lax.map(lambda frame: attend(frame[None])[0], qkv_a)
    branch = jnp.dot(spatial.reshape(frames * patches, width), w_out[0], preferred_element_type=jnp.float32)
    first = (flat.astype(jnp.float32) + mod_gate[0] * branch).astype(jnp.bfloat16)
    normed_b = modulate(first, mod_shift[1], mod_scale[1])
    qkv_b = jnp.dot(normed_b, w_qkv[1], preferred_element_type=jnp.float32).astype(jnp.bfloat16)
    by_patch = jnp.swapaxes(qkv_b.reshape(frames, patches, 3 * width), 0, 1)
    blocks = by_patch.reshape(patches // 8, 8, frames, 3 * width)
    temporal = lax.map(attend, blocks).reshape(patches, frames, width)
    temporal = jnp.swapaxes(temporal, 0, 1).reshape(frames * patches, width)
    branch = jnp.dot(temporal, w_out[1], preferred_element_type=jnp.float32)
    result = (first.astype(jnp.float32) + mod_gate[1] * branch).astype(jnp.bfloat16)
    return result.reshape(frames, patches, width)

def reference(tokens, w_qkv, w_out, mod_shift, mod_scale, mod_gate):
    return lax.map(lambda clip: one_clip(clip, w_qkv, w_out, mod_shift, mod_scale, mod_gate), tokens)
```

```python
import functools

import jax
import jax.numpy as jnp
from jax import lax
from jax.experimental import pallas as pl
from jax.experimental.pallas import tpu as pltpu
from jax.sharding import PartitionSpec as P

HEADS = 16
HEAD_DIM = 72
WIDTH = 1152
TOKENS = 256
THIRD = WIDTH // 3
LOG2E = 1.4426950408889634
MESH = pl.DeviceIdType.MESH

SLOT_ROWS = 144
QKV_COLS = 54
OUT_COLS = 18
PIECES = ((0, 48), (48, 32), (80, 32), (112, 32))
QKV_WINDOW = ((0, 0), (80, 10))
OUT_WINDOW = ((48, 6), (64, 8))


def normalise(values, shift, scale):
    mean = jnp.mean(values, axis=0, keepdims=True)
    centred = values - mean
    spread = jnp.mean(centred * centred, axis=0, keepdims=True)
    return (centred * lax.rsqrt(spread + 1e-06) * scale + shift).astype(jnp.bfloat16)


def kernel(
    x_ref, wqkv_ref, wout_ref, mod_ref, o_ref,
    slots, qkv, heads, mixed, xt, nt, ft, sel_out, sel_in,
    send_a, recv_a, send_b, recv_b,
    ring_send, ring_recv, opp_send, a2a_send, a2a_recv,
):
    dp = lax.axis_index("dp")
    seq = lax.axis_index("seq")
    core, xlo = dp % 2, dp // 2
    hi, z, y = seq // 32, (seq // 4) % 8, seq % 4
    other = 1 - core

    turn = (z + 24 - 3 * y) % 8
    place = other * (4 * z + (y + z) % 4) + core * (4 * (y + 4 * (turn // 4)) + turn % 4)

    def spot(n):
        n = (n + 64) % 32
        a, b = n // 4, n % 4
        zz = other * a + core * ((3 * a + b) % 8)
        yy = other * ((b + 32 - a) % 4) + core * (a % 4)
        return 4 * zz + yy

    def slot_of(n):
        return 32 * core + spot(n)

    forward = (dp, 32 * hi + spot(place + 1))
    backward = (dp, 32 * hi + spot(place + 31))
    sibling = (2 * xlo + other, seq)
    opposite = (2 * (1 - xlo) + core, 32 * (1 - hi) + 4 * z + y)
    own = 32 * core + 4 * z + y

    barrier = pltpu.get_barrier_semaphore()

    def greet(k, _):
        pl.semaphore_signal(barrier, inc=1, device_id=(dp, (seq + k) % 64), device_id_type=MESH)
        return 0

    lax.fori_loop(1, 64, greet, 0)
    pl.semaphore_signal(barrier, inc=1, device_id=sibling, device_id_type=MESH)
    pl.semaphore_signal(barrier, inc=1, device_id=opposite, device_id_type=MESH)

    rows = jnp.concatenate(
        [
            wqkv_ref[0].astype(jnp.float32).T,
            wout_ref[0].astype(jnp.float32).T,
            wout_ref[1].astype(jnp.float32).T,
            wqkv_ref[1].astype(jnp.float32).T,
        ],
        axis=0,
    ).astype(jnp.bfloat16)
    mine = 32 * hi + 4 * z + y
    slots[mine] = rows

    pl.semaphore_wait(barrier, 65)

    def part(slot, k):
        return slots.at[slot, pl.ds(PIECES[k][0], PIECES[k][1])]

    def push(slot, k, way, device):
        pltpu.make_async_remote_copy(
            src_ref=part(slot, k), dst_ref=part(slot, k),
            send_sem=ring_send.at[k, way], recv_sem=ring_recv.at[k, slot],
            device_id=device, device_id_type=MESH,
        ).start()

    def arrive(slot, k):
        pltpu.make_async_remote_copy(
            src_ref=part(slot, k), dst_ref=part(slot, k),
            send_sem=ring_send.at[k, 0], recv_sem=ring_recv.at[k, slot],
            device_id=sibling, device_id_type=MESH,
        ).wait_recv()

    def opp_copy(k):
        return pltpu.make_async_remote_copy(
            src_ref=part(mine, k), dst_ref=part(mine, k),
            send_sem=opp_send.at[k], recv_sem=ring_recv.at[k, mine],
            device_id=opposite, device_id_type=MESH,
        )

    @pl.when(hi == core)
    def _():
        for k in range(4):
            opp_copy(k).start()

    def ring_first(k):
        @pl.when(hi != core)
        def _():
            arrive(own, k)

        push(own, k, 0, forward)
        push(own, k, 1, backward)

        @pl.when(hi != core)
        def _():
            push(own, k, 2, sibling)

    def ring_steps(ks, lo, hi_):
        def step(t, _):
            for k in ks:
                slot = slot_of(place - t)
                arrive(slot, k)
                push(slot, k, 0, forward)
                push(slot, k, 2, sibling)
                slot = slot_of(place + t)
                arrive(slot, k)
                push(slot, k, 1, backward)
                push(slot, k, 2, sibling)
            return 0

        lax.fori_loop(lo, hi_, step, 0)

    def ring_last(ks):
        for k in ks:
            slot = slot_of(place - 15)
            arrive(slot, k)
            if k % 2 == 0:
                push(slot, k, 0, forward)
            push(slot, k, 2, sibling)
            slot = slot_of(place + 15)
            arrive(slot, k)
            if k % 2 == 1:
                push(slot, k, 1, backward)
            push(slot, k, 2, sibling)
        for k in ks:
            slot = slot_of(place + 16)
            arrive(slot, k)
            push(slot, k, 2, sibling)

    def from_sibling(ks):
        def step(t, _):
            slot = 32 * other + t
            for k in ks:

                @pl.when(jnp.logical_or(hi == core, t != 4 * z + y))
                def _():
                    arrive(slot, k)

            return 0

        lax.fori_loop(0, 32, step, 0)

    ring_first(0)
    ring_first(1)

    xt[...] = x_ref[...].astype(jnp.float32).T
    nt[...] = normalise(xt[...], mod_ref[:, 0:1], mod_ref[:, 2:3])

    def selection(shape, row_axis, by_frame):
        packed = lax.broadcasted_iota(jnp.int32, shape, row_axis)
        token = lax.broadcasted_iota(jnp.int32, shape, 1 - row_axis)
        s, r = packed // 16, packed % 16
        t, p = r // 4, r % 4
        at = 256 * t + (64 * p + s if by_frame else 4 * s + p)
        return jnp.where(jnp.logical_and(t < 3, at == token), 1.0, 0.0).astype(jnp.bfloat16)

    def pack(send_ref, by_frame):
        flat = jnp.concatenate([ft[0:THIRD], ft[THIRD : 2 * THIRD], ft[2 * THIRD :]], axis=1)
        packed = lax.dot_general(
            sel_out[by_frame], flat, (((1,), (1,)), ((), ())), preferred_element_type=jnp.float32
        )
        send_ref[...] = packed.astype(jnp.bfloat16).reshape(64, 16, THIRD)

    def unpack(recv_ref, by_frame):
        return jnp.dot(
            sel_in[by_frame], recv_ref[...].reshape(1024, THIRD), preferred_element_type=jnp.float32
        )

    for by_frame in (0, 1):
        sel_out[by_frame] = selection((1024, 768), 0, by_frame)
        sel_in[by_frame] = selection((768, 1024), 1, by_frame)

    def exchange(send_ref, recv_ref, which):
        def one(k, _):
            to = (seq + k) % 64
            pltpu.make_async_remote_copy(
                src_ref=send_ref.at[to], dst_ref=recv_ref.at[seq],
                send_sem=a2a_send.at[which], recv_sem=a2a_recv.at[which],
                device_id=(dp, to), device_id_type=MESH,
            ).start()
            return 0

        lax.fori_loop(1, 64, one, 0)
        recv_ref[seq] = send_ref[seq]

    def exchanged(send_ref, recv_ref, which):
        done = pltpu.make_async_remote_copy(
            src_ref=send_ref.at[pl.ds(0, 63)], dst_ref=recv_ref.at[pl.ds(0, 63)],
            send_sem=a2a_send.at[which], recv_sem=a2a_recv.at[which],
            device_id=sibling, device_id_type=MESH,
        )
        done.wait_send()
        done.wait_recv()

    def project_qkv(layer):
        first, offset = QKV_WINDOW[layer]

        def one(g, _):
            block = slots[pl.ds(8 * g, 8), pl.ds(first, 64)].reshape(512, WIDTH)
            got = jnp.dot(block, nt[...], preferred_element_type=jnp.float32)
            qkv[pl.ds(8 * g, 8)] = got.reshape(8, 64, TOKENS)
            return 0

        lax.fori_loop(0, 8, one, 0)

        def split(g, _):
            four = [qkv[4 * g + j] for j in range(4)]
            four = [f[offset : offset + QKV_COLS] for f in four]
            units = (
                jnp.concatenate([four[0], four[1][:18]], axis=0),
                jnp.concatenate([four[1][18:], four[2][:36]], axis=0),
                jnp.concatenate([four[2][36:], four[3]], axis=0),
            )
            for j, unit in enumerate(units):
                at = 3 * g + j
                factor = jnp.where(at < HEADS, HEAD_DIM**-0.5 * LOG2E, 1.0).astype(jnp.float32)
                heads[at] = (unit * factor).astype(jnp.bfloat16)
            return 0

        lax.fori_loop(0, 16, split, 0)

    def scores_of(h):
        return lax.dot_general(
            heads[HEADS + h], heads[h], (((0,), (0,)), ((), ())), preferred_element_type=jnp.float32
        )

    def mix(h, weights, total):
        got = jnp.dot(heads[2 * HEADS + h], weights, preferred_element_type=jnp.float32)
        mixed[pl.ds(pl.multiple_of(HEAD_DIM * h, 8), HEAD_DIM)] = got / total

    def attend_space(h):
        scores = scores_of(h)
        weights = jnp.exp2(scores - jnp.max(scores, axis=0, keepdims=True))
        total = jnp.sum(weights, axis=0, keepdims=True)
        mix(h, weights.astype(jnp.bfloat16), total)

    def attend_time(h):
        scores = scores_of(h)
        low = lax.broadcasted_iota(jnp.int32, (64, 128), 1) < 64
        near = jnp.concatenate(
            [
                jnp.where(low, scores[0:64, 0:128], scores[64:128, 0:128]),
                jnp.where(low, scores[128:192, 128:256], scores[192:256, 128:256]),
            ],
            axis=1,
        )
        weights = jnp.exp2(near - jnp.max(near, axis=0, keepdims=True))
        total = jnp.sum(weights, axis=0, keepdims=True)
        column = lax.broadcasted_iota(jnp.int32, (64, TOKENS), 1) // 64
        spread = jnp.concatenate([jnp.where(column == p, weights, 0.0) for p in range(4)], axis=0)
        mix(h, spread.astype(jnp.bfloat16), total)

    def project_out(layer):
        first, offset = OUT_WINDOW[layer]
        nt[...] = mixed[...].astype(jnp.bfloat16)

        def one(g, _):
            block = slots[pl.ds(8 * g, 8), pl.ds(first, 32)].reshape(256, WIDTH)
            got = jnp.dot(block, nt[...], preferred_element_type=jnp.float32).reshape(8, 32, TOKENS)
            got = jnp.concatenate([got[j, offset : offset + OUT_COLS] for j in range(8)], axis=0)
            at = pl.ds(pl.multiple_of(144 * g, 16), 144)
            ft[at] = (xt[at] + mod_ref[at, 4 + layer : 5 + layer] * got).astype(jnp.bfloat16)
            return 0

        lax.fori_loop(0, 8, one, 0)

    def over_heads(attend, lo, hi_):
        def one(h, _):
            attend(h)
            return 0

        lax.fori_loop(lo, hi_, one, 0)

    ring_steps((0, 1), 1, 15)
    ring_last((0, 1))
    ring_first(2)
    ring_first(3)
    from_sibling((0, 1))
    project_qkv(0)
    for q in range(4):
        over_heads(attend_space, 4 * q, 4 * q + 4)
        ring_steps((2, 3), 1 + q, 2 + q)
    project_out(0)
    pack(send_a, 0)
    exchange(send_a, recv_a, 0)
    ring_steps((2, 3), 5, 15)
    ring_last((2, 3))
    exchanged(send_a, recv_a, 0)

    got = unpack(recv_a, 1)
    for t in range(3):
        xt[THIRD * t : THIRD * (t + 1)] = got[TOKENS * t : TOKENS * (t + 1)].T
    nt[...] = normalise(xt[...], mod_ref[:, 1:2], mod_ref[:, 3:4])
    from_sibling((2, 3))
    project_qkv(1)
    over_heads(attend_time, 0, HEADS)
    project_out(1)
    pack(send_b, 1)
    exchange(send_b, recv_b, 1)
    exchanged(send_b, recv_b, 1)
    got = unpack(recv_b, 0)
    for t in range(3):
        o_ref[:, THIRD * t : THIRD * (t + 1)] = got[TOKENS * t : TOKENS * (t + 1)].astype(jnp.bfloat16)

    def sent(k, way, count):
        rows = pl.ds(PIECES[k][0], PIECES[k][1])
        pltpu.make_async_remote_copy(
            src_ref=slots.at[pl.ds(0, count), rows], dst_ref=slots.at[pl.ds(0, count), rows],
            send_sem=ring_send.at[k, way], recv_sem=ring_recv.at[k, 0],
            device_id=sibling, device_id_type=MESH,
        ).wait_send()

    for k in range(4):
        sent(k, 0, 16 - k % 2)
        sent(k, 1, 15 + k % 2)

        @pl.when(hi == core)
        def _():
            sent(k, 2, 31)
            opp_copy(k).wait_send()

        @pl.when(hi != core)
        def _():
            sent(k, 2, 32)


def per_device(tokens, w_qkv, w_out, mod_shift, mod_scale, mod_gate):
    mod = jnp.concatenate([mod_shift, mod_scale, mod_gate, jnp.zeros_like(mod_gate)], axis=0).T
    vmem = pl.BlockSpec(memory_space=pltpu.VMEM)
    result = pl.pallas_call(
        kernel,
        out_shape=jax.ShapeDtypeStruct((TOKENS, WIDTH), jnp.bfloat16),
        in_specs=[vmem] * 4,
        out_specs=vmem,
        scratch_shapes=[
            pltpu.VMEM((64, SLOT_ROWS, WIDTH), jnp.bfloat16),
            pltpu.VMEM((64, 64, TOKENS), jnp.float32),
            pltpu.VMEM((3 * HEADS, HEAD_DIM, TOKENS), jnp.bfloat16),
            pltpu.VMEM((WIDTH, TOKENS), jnp.float32),
            pltpu.VMEM((WIDTH, TOKENS), jnp.float32),
            pltpu.VMEM((WIDTH, TOKENS), jnp.bfloat16),
            pltpu.VMEM((WIDTH, TOKENS), jnp.bfloat16),
            pltpu.VMEM((2, 1024, 768), jnp.bfloat16),
            pltpu.VMEM((2, 768, 1024), jnp.bfloat16),
            pltpu.VMEM((64, 16, THIRD), jnp.bfloat16),
            pltpu.VMEM((64, 16, THIRD), jnp.bfloat16),
            pltpu.VMEM((64, 16, THIRD), jnp.bfloat16),
            pltpu.VMEM((64, 16, THIRD), jnp.bfloat16),
            pltpu.SemaphoreType.DMA((4, 3)),
            pltpu.SemaphoreType.DMA((4, 64)),
            pltpu.SemaphoreType.DMA((4,)),
            pltpu.SemaphoreType.DMA((2,)),
            pltpu.SemaphoreType.DMA((2,)),
        ],
        compiler_params=pltpu.CompilerParams(
            collective_id=0, has_side_effects=True, vmem_limit_bytes=60 * 2**20
        ),
        name="latte",
    )(tokens.reshape(TOKENS, WIDTH), w_qkv, w_out, mod)
    return result.reshape(tokens.shape)


def solution(mesh):
    in_specs = (
        P("dp", "seq", None, None),
        P(None, None, "seq"),
        P(None, None, "seq"),
        P(),
        P(),
        P(),
    )
    return jax.shard_map(
        per_device, mesh=mesh, in_specs=in_specs, out_specs=P("dp", "seq", None, None), check_vma=False
    )
```

```python
import functools

import jax
import jax.numpy as jnp
from jax import lax
from jax.experimental import pallas as pl
from jax.experimental.pallas import tpu as pltpu
from jax.sharding import PartitionSpec as P

HEADS = 16
HEAD_DIM = 72
WIDTH = 1152
TOKENS = 256
THIRD = WIDTH // 3
LOG2E = 1.4426950408889634
MESH = pl.DeviceIdType.MESH

SLOT_ROWS = 144
QKV_COLS = 54
OUT_COLS = 18
PIECES = (
    (0, 32, "z", False),
    (32, 16, "y", False),
    (48, 16, "z", True),
    (64, 16, "y", True),
    (80, 32, "z", False),
    (112, 16, "y", False),
    (128, 16, "y", True),
)
LAYER_PIECES = ((0, 1, 2, 3), (4, 5, 6))
ORDER = (
    32, 0, 64, 96, 33, 7, 71, 103, 1, 65, 24, 88, 39, 8, 56, 97, 40, 120, 72, 104, 6, 31, 2, 66,
    70, 34, 63, 38, 102, 98, 57, 112, 89, 16, 95, 47, 73, 25, 79, 80, 41, 5, 15, 48, 3, 127, 121, 111,
    30, 105, 67, 69, 14, 99, 10, 37, 35, 26, 94, 78, 58, 62, 101, 9, 23, 42, 46, 87, 49, 74, 122, 55,
    90, 126, 4, 119, 59, 110, 13, 106, 68, 17, 11, 81, 43, 113, 36, 123, 50, 18, 77, 29, 107, 27, 75, 91,
    100, 22, 60, 45, 54, 125, 86, 114, 61, 93, 82, 51, 28, 118, 12, 109, 21, 44, 53, 115, 76, 92, 19, 128,
    83, 160, 117, 192, 108, 124, 85, 20, 52, 84, 116, 135, 129, 152, 136, 199, 193, 167, 161, 216, 200, 184, 168, 159,
    153, 143, 134, 130, 137, 198, 166, 162, 144, 194, 223, 217, 191, 185, 208, 207, 176, 201, 142, 175, 169, 151, 138, 145,
    158, 133, 131, 197, 163, 154, 195, 222, 165, 186, 218, 215, 209, 190, 177, 150, 206, 202, 157, 170, 146, 183, 155, 174,
    141, 139, 187, 196, 132, 219, 164, 178, 210, 189, 171, 149, 221, 203, 182, 147, 188, 214, 173, 205, 156, 179, 172, 140,
    211, 181, 220, 213, 204, 212, 148, 180,
)
UP_Y, DOWN_Y, UP_Z, DOWN_Z, SIBLING, OPPOSITE = range(6)
QKV_WINDOW = ((0, 0), (80, 10))
OUT_WINDOW = ((48, 6), (64, 8))


def normalise(values, shift, scale):
    mean = jnp.mean(values, axis=0, keepdims=True)
    centred = values - mean
    spread = jnp.mean(centred * centred, axis=0, keepdims=True)
    return (centred * lax.rsqrt(spread + 1e-06) * scale + shift).astype(jnp.bfloat16)


def kernel(
    x_ref, wqkv_ref, wout_ref, shift_ref, scale_ref, gate_ref, o_ref,
    slots, mod, qkv, heads, mixed, xt, nt, ft, sel_out, sel_in,
    send_a, recv_a, send_b, recv_b,
    ring_send, ring_recv, a2a_send, a2a_recv,
):
    dp = lax.axis_index("dp")
    seq = lax.axis_index("seq")
    core, xlo = dp % 2, dp // 2
    hi, z, y = seq // 32, (seq // 4) % 8, seq % 4
    other = 1 - core

    def chip(yy, zz):
        return (dp, 32 * hi + 4 * ((zz + 8) % 8) + (yy + 4) % 4)

    sibling = (2 * xlo + other, seq)
    opposite = (2 * (1 - xlo) + core, 32 * (1 - hi) + 4 * z + y)
    devices = (chip(y + 1, z), chip(y - 1, z), chip(y, z + 1), chip(y, z - 1), sibling, opposite)

    barrier = pltpu.get_barrier_semaphore()

    def greet(k, _):
        pl.semaphore_signal(barrier, inc=1, device_id=(dp, (seq + k) % 64), device_id_type=MESH)
        return 0

    lax.fori_loop(1, 64, greet, 0)
    pl.semaphore_signal(barrier, inc=1, device_id=sibling, device_id_type=MESH)
    pl.semaphore_signal(barrier, inc=1, device_id=opposite, device_id_type=MESH)

    columns = wqkv_ref[...].astype(jnp.float32)
    outs = wout_ref[...].astype(jnp.float32)
    rows = jnp.concatenate([columns[:, 0], outs[:, 0], outs[:, 1], columns[:, 1]], axis=0).astype(jnp.bfloat16)
    mine = 32 * hi + 4 * z + y
    slots[mine] = rows

    pl.semaphore_wait(barrier, 65)

    def part(slot, k):
        return slots.at[slot, pl.ds(PIECES[k][0], PIECES[k][1])]

    def push(slot, k, way):
        pltpu.make_async_remote_copy(
            src_ref=part(slot, k), dst_ref=part(slot, k),
            send_sem=ring_send.at[k, way], recv_sem=ring_recv.at[k, slot],
            device_id=devices[way], device_id_type=MESH,
        ).start()

    def arrive(slot, k):
        pltpu.make_async_remote_copy(
            src_ref=part(slot, k), dst_ref=part(slot, k),
            send_sem=ring_send.at[k, 0], recv_sem=ring_recv.at[k, slot],
            device_id=sibling, device_id_type=MESH,
        ).wait_recv()

    def routes(k, dy, dz):
        ways = []
        if PIECES[k][2] == "z":
            if dy == 0:
                ways += {0: [UP_Z, DOWN_Z], 3: [DOWN_Z] * (k % 2), 4: [], 5: [UP_Z] * (1 - k % 2)}.get(
                    dz, [DOWN_Z] if dz < 4 else [UP_Z]
                )
                ways += [UP_Y, DOWN_Y]
            elif dy != 2 and (dz + k) % 2 == dy // 2:
                ways += [DOWN_Y if dy == 1 else UP_Y]
        else:
            if dz == 0:
                ways += [UP_Z, DOWN_Z]
                if dy == 0:
                    ways += [UP_Y, DOWN_Y]
                elif dy != 2 and k % 2 == dy // 2:
                    ways += [DOWN_Y if dy == 1 else UP_Y]
            elif dz in (3, 5):
                if (dy + k) % 2 == dz // 4:
                    ways += [DOWN_Z if dz == 3 else UP_Z]
            elif dz != 4:
                ways += [DOWN_Z if dz < 4 else UP_Z]
        return ways

    def block_of(half, dy, dz):
        return 32 * half + 4 * lax.rem(z + dz, 8) + lax.rem(y + dy, 4)

    def event(k, dy, dz):
        slot = block_of(core, dy, dz)
        last = PIECES[k][3]
        start = dy == 0 and dz == 0

        def onward():
            for way in routes(k, dy, dz):
                push(slot, k, way)

        if start:

            @pl.when(hi != core)
            def _():
                arrive(slot, k)

            @pl.when(hi == core)
            def _():
                push(slot, k, OPPOSITE)
                if last:
                    onward()

            @pl.when(hi != core)
            def _():
                push(slot, k, SIBLING)

        else:
            arrive(slot, k)
            if last:

                @pl.when(hi == core)
                def _():
                    onward()
                    push(slot, k, OPPOSITE)

            push(slot, k, SIBLING)
        if not last:
            onward()

    def course(k):
        return [(k, dy, dz) for dy in range(4) for dz in range(8)]

    def run(events):
        for e in events:
            event(*e)

    def from_sibling(ks, dy, dz):
        slot = block_of(other, dy, dz)

        def taken():
            for k in ks:
                arrive(slot, k)

        if dy == 0 and dz == 0:
            pl.when(hi == core)(taken)
        else:
            taken()

    order = [(e // 32, e // 8 % 4, e % 8) for e in ORDER]
    end_a = 1 + max(i for i, e in enumerate(order) if e[0] in LAYER_PIECES[0])
    run(order[:4])

    def prepare():
        six = jnp.concatenate([shift_ref[...], scale_ref[...], gate_ref[...], gate_ref[...]], axis=0)
        mod[...] = six.T
        xt[...] = x_ref[...].astype(jnp.float32).T
        nt[...] = normalise(xt[...], mod[:, 0:1], mod[:, 2:3])

    def selected(shape, axis, start, by_frame):
        packed = lax.broadcasted_iota(jnp.int32, shape, axis) + start
        s, t, p = packed >> 4, (packed >> 2) & 3, packed & 3
        at = 256 * t + (64 * p + s if by_frame else 4 * s + p)
        return jnp.where(t < 3, at, -1)

    def make_sel_out(by_frame, q):
        at = selected((256, 1), 0, 256 * q, by_frame)
        token = lax.broadcasted_iota(jnp.int32, (256, 768), 1)
        sel_out[by_frame, 256 * q : 256 * (q + 1)] = jnp.where(at == token, 1.0, 0.0).astype(jnp.bfloat16)

    def make_sel_in(by_frame, q):
        at = selected((1, 1024), 1, 0, by_frame)
        token = lax.broadcasted_iota(jnp.int32, (256, 1024), 0) + 256 * q
        sel_in[by_frame, 256 * q : 256 * (q + 1)] = jnp.where(at == token, 1.0, 0.0).astype(jnp.bfloat16)

    def pack_and_send(send_ref, recv_ref, by_frame):
        flat = jnp.concatenate([ft[0:THIRD], ft[THIRD : 2 * THIRD], ft[2 * THIRD :]], axis=1)

        def quarter(c, _):
            q = lax.rem(seq // 16 + 1 + c, 4)
            packed = lax.dot_general(
                sel_out[by_frame, pl.ds(pl.multiple_of(256 * q, 256), 256)], flat,
                (((1,), (1,)), ((), ())), preferred_element_type=jnp.float32,
            )
            send_ref[pl.ds(16 * q, 16)] = packed.astype(jnp.bfloat16).reshape(16, 16, THIRD)

            def one(j, _):
                to = 16 * q + lax.rem(seq + j, 16)

                @pl.when(to != seq)
                def _():
                    pltpu.make_async_remote_copy(
                        src_ref=send_ref.at[to], dst_ref=recv_ref.at[seq],
                        send_sem=a2a_send.at[by_frame], recv_sem=a2a_recv.at[by_frame],
                        device_id=(dp, to), device_id_type=MESH,
                    ).start()

                return 0

            lax.fori_loop(0, 16, one, 0)
            return 0

        lax.fori_loop(0, 4, quarter, 0)
        recv_ref[seq] = send_ref[seq]

    def unpack(recv_ref, by_frame):
        return jnp.dot(
            sel_in[by_frame], recv_ref[...].reshape(1024, THIRD), preferred_element_type=jnp.float32
        )

    def exchanged(send_ref, recv_ref, which):
        done = pltpu.make_async_remote_copy(
            src_ref=send_ref.at[pl.ds(0, 63)], dst_ref=recv_ref.at[pl.ds(0, 63)],
            send_sem=a2a_send.at[which], recv_sem=a2a_recv.at[which],
            device_id=sibling, device_id_type=MESH,
        )
        done.wait_send()
        done.wait_recv()

    def project_slots(layer, slot_list):
        first = QKV_WINDOW[layer][0]
        block = jnp.concatenate([slots[j, pl.ds(first, 64)] for j in slot_list], axis=0)
        got = jnp.dot(block, nt[...], preferred_element_type=jnp.float32)
        for n, j in enumerate(slot_list):
            qkv[j] = got[64 * n : 64 * (n + 1)]

    def project_qkv(layer):
        def one(g, _):
            project_slots(layer, [8 * g + j for j in range(8)])
            return 0

        lax.fori_loop(0, 8, one, 0)

    def split_heads(layer, lo, hi_):
        offset = QKV_WINDOW[layer][1]

        def split(g, _):
            four = [qkv[4 * g + j, offset : offset + QKV_COLS] for j in range(4)]
            units = (
                jnp.concatenate([four[0], four[1][:18]], axis=0),
                jnp.concatenate([four[1][18:], four[2][:36]], axis=0),
                jnp.concatenate([four[2][36:], four[3]], axis=0),
            )
            for j, unit in enumerate(units):
                at = 3 * g + j
                factor = jnp.where(at < HEADS, HEAD_DIM**-0.5 * LOG2E, 1.0).astype(jnp.float32)
                heads[at] = (unit * factor).astype(jnp.bfloat16)
            return 0

        lax.fori_loop(lo, hi_, split, 0)

    def scores_of(h):
        return lax.dot_general(
            heads[HEADS + h], heads[h], (((0,), (0,)), ((), ())), preferred_element_type=jnp.float32
        )

    def mix(h, weights, total):
        got = jnp.dot(heads[2 * HEADS + h], weights, preferred_element_type=jnp.float32)
        mixed[pl.ds(pl.multiple_of(HEAD_DIM * h, 8), HEAD_DIM)] = got / total

    def attend_space(h):
        scores = scores_of(h)
        weights = jnp.exp2(scores - jnp.max(scores, axis=0, keepdims=True))
        total = jnp.sum(weights, axis=0, keepdims=True)
        mix(h, weights.astype(jnp.bfloat16), total)

    def attend_time(h):
        scores = scores_of(h)
        low = lax.broadcasted_iota(jnp.int32, (64, 128), 1) < 64
        near = jnp.concatenate(
            [
                jnp.where(low, scores[0:64, 0:128], scores[64:128, 0:128]),
                jnp.where(low, scores[128:192, 128:256], scores[192:256, 128:256]),
            ],
            axis=1,
        )
        weights = jnp.exp2(near - jnp.max(near, axis=0, keepdims=True))
        total = jnp.sum(weights, axis=0, keepdims=True)
        column = lax.broadcasted_iota(jnp.int32, (64, TOKENS), 1) // 64
        spread = jnp.concatenate([jnp.where(column == p, weights, 0.0) for p in range(4)], axis=0)
        mix(h, spread.astype(jnp.bfloat16), total)

    def project_out(layer, lo, hi_):
        first, offset = OUT_WINDOW[layer]

        def one(g, _):
            block = slots[pl.ds(8 * g, 8), pl.ds(first, 32)].reshape(256, WIDTH)
            got = jnp.dot(block, nt[...], preferred_element_type=jnp.float32).reshape(8, 32, TOKENS)
            got = jnp.concatenate([got[j, offset : offset + OUT_COLS] for j in range(8)], axis=0)
            at = pl.ds(pl.multiple_of(144 * g, 16), 144)
            ft[at] = (xt[at] + mod[at, 4 + layer : 5 + layer] * got).astype(jnp.bfloat16)
            return 0

        lax.fori_loop(lo, hi_, one, 0)

    def over_heads(attend, lo, hi_):
        def one(n, _):
            attend(lo + 2 * n)
            attend(lo + 2 * n + 1)
            return 0

        lax.fori_loop(0, (hi_ - lo) // 2, one, 0)

    done = {}
    for i, (k, dy, dz) in enumerate(order[:end_a]):
        if k in LAYER_PIECES[0]:
            done[dy, dz] = i
    blocks = sorted(done, key=done.get)
    batches = [blocks[n : n + 4] for n in range(0, 32, 4)]
    after = {}
    tasks = [functools.partial(make_sel_out, 0, q) for q in range(4)]
    tasks += [functools.partial(make_sel_in, 1, q) for q in range(3)]
    tasks += [functools.partial(make_sel_out, 1, q) for q in range(4)]
    tasks += [functools.partial(make_sel_in, 0, q) for q in range(3)]
    for n, task in enumerate([prepare] + tasks):
        after.setdefault(6 + 4 * n, []).append(task)

    def batch(n):
        ready = [block_of(core, dy, dz) for dy, dz in batches[n]] if n < 8 else []
        if n > 0:
            for dy, dz in batches[n - 1]:
                from_sibling(LAYER_PIECES[0], dy, dz)
                ready.append(block_of(other, dy, dz))
        project_slots(0, ready)

    for n in range(8):
        after.setdefault(max(done[block] for block in batches[n]), []).append(functools.partial(batch, n))
    for i in range(4, end_a):
        run(order[i : i + 1])
        for task in after.get(i, []):
            task()
    batch(8)

    rest = order[end_a:]

    def more(count):
        run(rest[:count])
        del rest[:count]

    for q in range(4):
        split_heads(0, 4 * q, 4 * q + 4)
        more(2)
    for q in range(8):
        over_heads(attend_space, 2 * q, 2 * q + 2)
        more(3)
    nt[...] = mixed[...].astype(jnp.bfloat16)
    for q in range(4):
        project_out(0, 2 * q, 2 * q + 2)
        more(3)
    pack_and_send(send_a, recv_a, 0)
    more(len(rest))
    for dy in range(4):
        for dz in range(8):
            from_sibling(LAYER_PIECES[1], dy, dz)
    exchanged(send_a, recv_a, 0)

    got = unpack(recv_a, 1)
    for t in range(3):
        xt[THIRD * t : THIRD * (t + 1)] = got[TOKENS * t : TOKENS * (t + 1)].T
    nt[...] = normalise(xt[...], mod[:, 1:2], mod[:, 3:4])
    project_qkv(1)
    split_heads(1, 0, 16)
    over_heads(attend_time, 0, HEADS)
    nt[...] = mixed[...].astype(jnp.bfloat16)
    project_out(1, 0, 8)
    pack_and_send(send_b, recv_b, 1)
    exchanged(send_b, recv_b, 1)
    got = unpack(recv_b, 0)
    for t in range(3):
        o_ref[:, THIRD * t : THIRD * (t + 1)] = got[TOKENS * t : TOKENS * (t + 1)].astype(jnp.bfloat16)

    def sent(k, way, count):
        rows = pl.ds(PIECES[k][0], PIECES[k][1])
        pltpu.make_async_remote_copy(
            src_ref=slots.at[pl.ds(0, count), rows], dst_ref=slots.at[pl.ds(0, count), rows],
            send_sem=ring_send.at[k, way], recv_sem=ring_recv.at[k, 0],
            device_id=sibling, device_id_type=MESH,
        ).wait_send()

    for k, piece in enumerate(PIECES):
        ways = [way for e in course(k) for way in routes(*e)]

        def plane_sent():
            for way in (UP_Y, DOWN_Y, UP_Z, DOWN_Z):
                sent(k, way, ways.count(way))

        if not piece[3]:
            plane_sent()

        @pl.when(hi == core)
        def _():
            if piece[3]:
                plane_sent()
            sent(k, OPPOSITE, 32 if piece[3] else 1)
            sent(k, SIBLING, 31)

        @pl.when(hi != core)
        def _():
            sent(k, SIBLING, 32)


def per_device(tokens, w_qkv, w_out, mod_shift, mod_scale, mod_gate):
    vmem = pl.BlockSpec(memory_space=pltpu.VMEM)
    result = pl.pallas_call(
        kernel,
        out_shape=jax.ShapeDtypeStruct((TOKENS, WIDTH), jnp.bfloat16),
        in_specs=[vmem] * 6,
        out_specs=vmem,
        scratch_shapes=[
            pltpu.VMEM((64, SLOT_ROWS, WIDTH), jnp.bfloat16),
            pltpu.VMEM((WIDTH, 8), jnp.float32),
            pltpu.VMEM((64, 64, TOKENS), jnp.float32),
            pltpu.VMEM((3 * HEADS, HEAD_DIM, TOKENS), jnp.bfloat16),
            pltpu.VMEM((WIDTH, TOKENS), jnp.float32),
            pltpu.VMEM((WIDTH, TOKENS), jnp.float32),
            pltpu.VMEM((WIDTH, TOKENS), jnp.bfloat16),
            pltpu.VMEM((WIDTH, TOKENS), jnp.bfloat16),
            pltpu.VMEM((2, 1024, 768), jnp.bfloat16),
            pltpu.VMEM((2, 768, 1024), jnp.bfloat16),
            pltpu.VMEM((64, 16, THIRD), jnp.bfloat16),
            pltpu.VMEM((64, 16, THIRD), jnp.bfloat16),
            pltpu.VMEM((64, 16, THIRD), jnp.bfloat16),
            pltpu.VMEM((64, 16, THIRD), jnp.bfloat16),
            pltpu.SemaphoreType.DMA((len(PIECES), 6)),
            pltpu.SemaphoreType.DMA((len(PIECES), 64)),
            pltpu.SemaphoreType.DMA((2,)),
            pltpu.SemaphoreType.DMA((2,)),
        ],
        compiler_params=pltpu.CompilerParams(
            collective_id=0, has_side_effects=True, vmem_limit_bytes=60 * 2**20
        ),
        name="latte",
    )(
        tokens.reshape(TOKENS, WIDTH),
        jnp.transpose(w_qkv, (2, 0, 1)),
        jnp.transpose(w_out, (2, 0, 1)),
        mod_shift,
        mod_scale,
        mod_gate,
    )
    return result.reshape(tokens.shape)


def solution(mesh):
    in_specs = (
        P("dp", "seq", None, None),
        P(None, None, "seq"),
        P(None, None, "seq"),
        P(),
        P(),
        P(),
    )
    return jax.shard_map(
        per_device, mesh=mesh, in_specs=in_specs, out_specs=P("dp", "seq", None, None), check_vma=False
    )
```

```python
import functools

import jax
import jax.numpy as jnp
from jax import lax
from jax.experimental import pallas as pl
from jax.experimental.pallas import tpu as pltpu
from jax.sharding import PartitionSpec as P

HEADS = 16
HEAD_DIM = 72
WIDTH = 1152
TOKENS = 256
THIRD = WIDTH // 3
LOG2E = 1.4426950408889634
MESH = pl.DeviceIdType.MESH

SLOT_ROWS = 144
QKV_COLS = 54
OUT_COLS = 18
PIECES = (
    (0, 32, "z", False),
    (32, 16, "y", False),
    (48, 16, "z", True),
    (64, 16, "y", True),
    (80, 32, "z", False),
    (112, 16, "y", False),
    (128, 16, "y", True),
)
GROUPS = ((0, 1, 2, 3), (), (4, 5, 6))
ORDER = (
    32, 0, 64, 96, 33, 7, 71, 103, 1, 39, 88, 65, 24, 8, 97, 56, 120, 40, 72, 104, 6, 2, 31, 66,
    70, 34, 63, 38, 98, 25, 57, 89, 112, 16, 102, 95, 47, 79, 80, 73, 41, 48, 15, 5, 3, 127, 121, 111,
    30, 67, 14, 10, 26, 105, 37, 9, 69, 35, 94, 78, 23, 58, 62, 101, 42, 99, 46, 49, 90, 74, 122, 55,
    126, 87, 119, 59, 110, 4, 81, 106, 113, 13, 68, 11, 17, 36, 22, 50, 29, 43, 123, 77, 18, 27, 91, 60,
    100, 45, 75, 86, 54, 107, 114, 61, 93, 82, 51, 28, 118, 12, 109, 125, 21, 53, 115, 76, 19, 44, 128, 124,
    160, 92, 192, 117, 83, 20, 85, 52, 108, 84, 116, 135, 129, 152, 136, 199, 193, 167, 161, 216, 200, 184, 168, 159,
    153, 143, 134, 130, 137, 198, 166, 162, 144, 194, 223, 217, 191, 185, 208, 207, 176, 201, 142, 175, 169, 151, 138, 145,
    158, 133, 131, 197, 163, 154, 195, 222, 165, 186, 218, 215, 209, 190, 177, 150, 206, 202, 157, 170, 146, 183, 155, 174,
    141, 139, 187, 196, 132, 219, 164, 178, 210, 189, 171, 149, 221, 203, 182, 147, 188, 214, 173, 205, 156, 179, 172, 140,
    211, 181, 220, 213, 204, 212, 148, 180,
)
UP_Y, DOWN_Y, UP_Z, DOWN_Z, SIBLING, OPPOSITE = range(6)
QKV_WINDOW = ((0, 0), (80, 10))
OUT_WINDOW = ((48, 6), (64, 8))


def normalise(values, shift, scale):
    mean = jnp.mean(values, axis=0, keepdims=True)
    centred = values - mean
    spread = jnp.mean(centred * centred, axis=0, keepdims=True)
    return (centred * lax.rsqrt(spread + 1e-06) * scale + shift).astype(jnp.bfloat16)


def kernel(
    x_ref, wqkv_ref, wout_ref, shift_ref, scale_ref, gate_ref, o_ref,
    slots, mod, qkv, heads, mixed, xt, nt, ft, sel_out, sel_in,
    send_a, recv_a, send_b, recv_b,
    ring_send, ring_recv, a2a_send, a2a_recv, entered,
):
    dp = lax.axis_index("dp")
    seq = lax.axis_index("seq")
    core, xlo = dp % 2, dp // 2
    hi, z, y = seq // 32, (seq // 4) % 8, seq % 4
    other = 1 - core

    def chip(yy, zz):
        return (dp, 32 * hi + 4 * ((zz + 8) % 8) + (yy + 4) % 4)

    sibling = (2 * xlo + other, seq)
    opposite = (2 * (1 - xlo) + core, 32 * (1 - hi) + 4 * z + y)
    beside = (2 * (1 - xlo) + core, seq)
    devices = (chip(y + 1, z), chip(y - 1, z), chip(y, z + 1), chip(y, z - 1), sibling, opposite)

    barrier = pltpu.get_barrier_semaphore()

    for device in (*devices, beside):
        pl.semaphore_signal(barrier, inc=1, device_id=device, device_id_type=MESH)

    columns = wqkv_ref[...].astype(jnp.float32)
    outs = wout_ref[...].astype(jnp.float32)
    rows = jnp.concatenate([columns[:, 0], outs[:, 0], outs[:, 1], columns[:, 1]], axis=0).astype(jnp.bfloat16)
    mine = 32 * hi + 4 * z + y
    slots[mine] = rows

    pl.semaphore_wait(barrier, 7)

    def part(slot, k):
        return slots.at[slot, pl.ds(PIECES[k][0], PIECES[k][1])]

    def push(slot, k, way):
        pltpu.make_async_remote_copy(
            src_ref=part(slot, k), dst_ref=part(slot, k),
            send_sem=ring_send.at[k, way], recv_sem=ring_recv.at[k, slot],
            device_id=devices[way], device_id_type=MESH,
        ).start()

    def arrive(slot, k):
        pltpu.make_async_remote_copy(
            src_ref=part(slot, k), dst_ref=part(slot, k),
            send_sem=ring_send.at[k, 0], recv_sem=ring_recv.at[k, slot],
            device_id=sibling, device_id_type=MESH,
        ).wait_recv()

    def routes(k, dy, dz):
        ways = []
        if PIECES[k][2] == "z":
            if dy == 0:
                ways += {0: [UP_Z, DOWN_Z], 3: [DOWN_Z] * (k % 2), 4: [], 5: [UP_Z] * (1 - k % 2)}.get(
                    dz, [DOWN_Z] if dz < 4 else [UP_Z]
                )
                ways += [UP_Y, DOWN_Y]
            elif dy != 2 and (dz + k) % 2 == dy // 2:
                ways += [DOWN_Y if dy == 1 else UP_Y]
        else:
            if dz == 0:
                ways += [UP_Z, DOWN_Z]
                if dy == 0:
                    ways += [UP_Y, DOWN_Y]
                elif dy != 2 and k % 2 == dy // 2:
                    ways += [DOWN_Y if dy == 1 else UP_Y]
            elif dz in (3, 5):
                if (dy + k) % 2 == dz // 4:
                    ways += [DOWN_Z if dz == 3 else UP_Z]
            elif dz != 4:
                ways += [DOWN_Z if dz < 4 else UP_Z]
        return ways

    def block_of(half, dy, dz):
        return 32 * half + 4 * lax.rem(z + dz, 8) + lax.rem(y + dy, 4)

    def event(k, dy, dz):
        slot = block_of(core, dy, dz)
        last = PIECES[k][3]
        start = dy == 0 and dz == 0

        def onward():
            for way in routes(k, dy, dz):
                push(slot, k, way)

        if start:

            @pl.when(hi != core)
            def _():
                arrive(slot, k)

            @pl.when(hi == core)
            def _():
                push(slot, k, OPPOSITE)
                if last:
                    onward()

            @pl.when(hi != core)
            def _():
                push(slot, k, SIBLING)

        else:
            arrive(slot, k)
            if last:

                @pl.when(hi == core)
                def _():
                    onward()
                    push(slot, k, OPPOSITE)

            push(slot, k, SIBLING)
        if not last:
            onward()

    def course(k):
        return [(k, dy, dz) for dy in range(4) for dz in range(8)]

    def run(events):
        for e in events:
            event(*e)

    def from_sibling(ks, dy, dz):
        slot = block_of(other, dy, dz)

        def taken():
            for k in ks:
                arrive(slot, k)

        if dy == 0 and dz == 0:
            pl.when(hi == core)(taken)
        else:
            taken()

    def all_from_sibling(ks):
        for dy in range(4):
            for dz in range(8):
                from_sibling(ks, dy, dz)

    order = [(e // 32, e // 8 % 4, e % 8) for e in ORDER]
    end_a = 1 + max(i for i, e in enumerate(order) if e[0] in GROUPS[0])
    run(order[:4])

    def prepare():
        six = jnp.concatenate([shift_ref[...], scale_ref[...], gate_ref[...], gate_ref[...]], axis=0)
        mod[...] = six.T
        xt[...] = x_ref[...].astype(jnp.float32).T
        nt[...] = normalise(xt[...], mod[:, 0:1], mod[:, 2:3])

    def selected(shape, axis, start, by_frame):
        packed = lax.broadcasted_iota(jnp.int32, shape, axis) + start
        s, t, p = packed >> 4, (packed >> 2) & 3, packed & 3
        at = 256 * t + (64 * p + s if by_frame else 4 * s + p)
        return jnp.where(t < 3, at, -1)

    def make_sel_out(by_frame, q):
        at = selected((256, 1), 0, 256 * q, by_frame)
        token = lax.broadcasted_iota(jnp.int32, (256, 768), 1)
        sel_out[by_frame, 256 * q : 256 * (q + 1)] = jnp.where(at == token, 1.0, 0.0).astype(jnp.bfloat16)

    def make_sel_in(by_frame, q):
        at = selected((1, 1024), 1, 0, by_frame)
        token = lax.broadcasted_iota(jnp.int32, (256, 1024), 0) + 256 * q
        sel_in[by_frame, 256 * q : 256 * (q + 1)] = jnp.where(at == token, 1.0, 0.0).astype(jnp.bfloat16)

    def pack_and_send(send_ref, recv_ref, by_frame):
        flat = jnp.concatenate([ft[0:THIRD], ft[THIRD : 2 * THIRD], ft[2 * THIRD :]], axis=1)

        def quarter(c, _):
            q = lax.rem(seq // 16 + 1 + c, 4)
            packed = lax.dot_general(
                sel_out[by_frame, pl.ds(pl.multiple_of(256 * q, 256), 256)], flat,
                (((1,), (1,)), ((), ())), preferred_element_type=jnp.float32,
            )
            send_ref[pl.ds(16 * q, 16)] = packed.astype(jnp.bfloat16).reshape(16, 16, THIRD)

            def one(j, _):
                to = 16 * q + lax.rem(seq + j, 16)

                @pl.when(to != seq)
                def _():
                    pltpu.make_async_remote_copy(
                        src_ref=send_ref.at[to], dst_ref=recv_ref.at[seq],
                        send_sem=a2a_send.at[by_frame], recv_sem=a2a_recv.at[by_frame],
                        device_id=(dp, to), device_id_type=MESH,
                    ).start()

                return 0

            lax.fori_loop(0, 16, one, 0)
            return 0

        lax.fori_loop(0, 4, quarter, 0)
        recv_ref[seq] = send_ref[seq]

    def unpack(recv_ref, by_frame):
        return jnp.dot(
            sel_in[by_frame], recv_ref[...].reshape(1024, THIRD), preferred_element_type=jnp.float32
        )

    def exchanged(send_ref, recv_ref, which):
        done = pltpu.make_async_remote_copy(
            src_ref=send_ref.at[pl.ds(0, 63)], dst_ref=recv_ref.at[pl.ds(0, 63)],
            send_sem=a2a_send.at[which], recv_sem=a2a_recv.at[which],
            device_id=sibling, device_id_type=MESH,
        )
        done.wait_send()
        done.wait_recv()

    def project_slots(layer, slot_list):
        first = QKV_WINDOW[layer][0]
        block = jnp.concatenate([slots[j, pl.ds(first, 64)] for j in slot_list], axis=0)
        got = jnp.dot(block, nt[...], preferred_element_type=jnp.float32)
        for n, j in enumerate(slot_list):
            qkv[j] = got[64 * n : 64 * (n + 1)]

    def project_qkv(layer):
        def one(g, _):
            project_slots(layer, [8 * g + j for j in range(8)])
            return 0

        lax.fori_loop(0, 8, one, 0)

    def split_heads(layer, lo, hi_):
        offset = QKV_WINDOW[layer][1]

        def split(g, _):
            four = [qkv[4 * g + j, offset : offset + QKV_COLS] for j in range(4)]
            units = (
                jnp.concatenate([four[0], four[1][:18]], axis=0),
                jnp.concatenate([four[1][18:], four[2][:36]], axis=0),
                jnp.concatenate([four[2][36:], four[3]], axis=0),
            )
            for j, unit in enumerate(units):
                at = 3 * g + j
                factor = jnp.where(at < HEADS, HEAD_DIM**-0.5 * LOG2E, 1.0).astype(jnp.float32)
                heads[at] = (unit * factor).astype(jnp.bfloat16)
            return 0

        lax.fori_loop(lo, hi_, split, 0)

    def scores_of(h):
        return lax.dot_general(
            heads[HEADS + h], heads[h], (((0,), (0,)), ((), ())), preferred_element_type=jnp.float32
        )

    def mix(h, weights, total):
        got = jnp.dot(heads[2 * HEADS + h], weights, preferred_element_type=jnp.float32)
        mixed[pl.ds(pl.multiple_of(HEAD_DIM * h, 8), HEAD_DIM)] = got / total

    def attend_space(h):
        scores = scores_of(h)
        weights = jnp.exp2(scores - jnp.max(scores, axis=0, keepdims=True))
        total = jnp.sum(weights, axis=0, keepdims=True)
        mix(h, weights.astype(jnp.bfloat16), total)

    def attend_time(h):
        scores = scores_of(h)
        low = lax.broadcasted_iota(jnp.int32, (64, 128), 1) < 64
        near = jnp.concatenate(
            [
                jnp.where(low, scores[0:64, 0:128], scores[64:128, 0:128]),
                jnp.where(low, scores[128:192, 128:256], scores[192:256, 128:256]),
            ],
            axis=1,
        )
        weights = jnp.exp2(near - jnp.max(near, axis=0, keepdims=True))
        total = jnp.sum(weights, axis=0, keepdims=True)
        column = lax.broadcasted_iota(jnp.int32, (64, TOKENS), 1) // 64
        spread = jnp.concatenate([jnp.where(column == p, weights, 0.0) for p in range(4)], axis=0)
        mix(h, spread.astype(jnp.bfloat16), total)

    def project_out(layer, lo, hi_):
        first, offset = OUT_WINDOW[layer]

        def one(g, _):
            block = slots[pl.ds(8 * g, 8), pl.ds(first, 32)].reshape(256, WIDTH)
            got = jnp.dot(block, nt[...], preferred_element_type=jnp.float32).reshape(8, 32, TOKENS)
            got = jnp.concatenate([got[j, offset : offset + OUT_COLS] for j in range(8)], axis=0)
            at = pl.ds(pl.multiple_of(144 * g, 16), 144)
            ft[at] = (xt[at] + mod[at, 4 + layer : 5 + layer] * got).astype(jnp.bfloat16)
            return 0

        lax.fori_loop(lo, hi_, one, 0)

    def over_heads(attend, lo, hi_):
        def one(n, _):
            attend(lo + 2 * n)
            attend(lo + 2 * n + 1)
            return 0

        lax.fori_loop(0, (hi_ - lo) // 2, one, 0)

    done = {}
    for i, (k, dy, dz) in enumerate(order[:end_a]):
        if k in GROUPS[0]:
            done[dy, dz] = i
    blocks = sorted(done, key=done.get)
    batches = [blocks[n : n + 4] for n in range(0, 32, 4)]
    after = {}
    tasks = [functools.partial(make_sel_out, 0, q) for q in range(4)]
    tasks += [functools.partial(make_sel_in, 1, q) for q in range(3)]
    tasks += [functools.partial(make_sel_out, 1, q) for q in range(4)]
    tasks += [functools.partial(make_sel_in, 0, q) for q in range(3)]
    for n, task in enumerate([prepare] + tasks):
        after.setdefault(6 + 4 * n, []).append(task)

    def batch(n):
        ready = [block_of(core, dy, dz) for dy, dz in batches[n]] if n < 8 else []
        if n > 0:
            for dy, dz in batches[n - 1]:
                from_sibling(GROUPS[0], dy, dz)
                ready.append(block_of(other, dy, dz))
        project_slots(0, ready)

    for n in range(8):
        after.setdefault(max(done[block] for block in batches[n]), []).append(functools.partial(batch, n))
    for i in range(4, end_a):
        run(order[i : i + 1])
        for task in after.get(i, []):
            task()
    batch(8)

    def tell(n, device):
        pl.semaphore_signal(entered.at[n], inc=1, device_id=device, device_id_type=MESH)

    tell(0, opposite)

    rest = order[end_a:]

    def more(count):
        run(rest[:count])
        del rest[:count]

    for q in range(4):
        split_heads(0, 4 * q, 4 * q + 4)
        more(4)
    for q in range(8):
        over_heads(attend_space, 2 * q, 2 * q + 2)
        more(5)
    pl.semaphore_wait(entered.at[0], 1)
    tell(1, beside)
    if GROUPS[1]:
        more(1 + max([i for i, e in enumerate(rest) if e[0] in GROUPS[1]], default=-1))
        all_from_sibling(GROUPS[1])
    nt[...] = mixed[...].astype(jnp.bfloat16)
    for q in range(4):
        project_out(0, 2 * q, 2 * q + 2)
        more(4)
    pl.semaphore_wait(entered.at[1], 1)
    pack_and_send(send_a, recv_a, 0)
    more(len(rest))
    all_from_sibling(GROUPS[2])
    exchanged(send_a, recv_a, 0)

    got = unpack(recv_a, 1)
    for t in range(3):
        xt[THIRD * t : THIRD * (t + 1)] = got[TOKENS * t : TOKENS * (t + 1)].T
    nt[...] = normalise(xt[...], mod[:, 1:2], mod[:, 3:4])
    project_qkv(1)
    split_heads(1, 0, 16)
    over_heads(attend_time, 0, HEADS)
    nt[...] = mixed[...].astype(jnp.bfloat16)
    project_out(1, 0, 8)
    pack_and_send(send_b, recv_b, 1)
    exchanged(send_b, recv_b, 1)
    got = unpack(recv_b, 0)
    for t in range(3):
        o_ref[:, THIRD * t : THIRD * (t + 1)] = got[TOKENS * t : TOKENS * (t + 1)].astype(jnp.bfloat16)

    def sent(k, way, count):
        rows = pl.ds(PIECES[k][0], PIECES[k][1])
        pltpu.make_async_remote_copy(
            src_ref=slots.at[pl.ds(0, count), rows], dst_ref=slots.at[pl.ds(0, count), rows],
            send_sem=ring_send.at[k, way], recv_sem=ring_recv.at[k, 0],
            device_id=sibling, device_id_type=MESH,
        ).wait_send()

    for k, piece in enumerate(PIECES):
        ways = [way for e in course(k) for way in routes(*e)]

        def plane_sent():
            for way in (UP_Y, DOWN_Y, UP_Z, DOWN_Z):
                sent(k, way, ways.count(way))

        if not piece[3]:
            plane_sent()

        @pl.when(hi == core)
        def _():
            if piece[3]:
                plane_sent()
            sent(k, OPPOSITE, 32 if piece[3] else 1)
            sent(k, SIBLING, 31)

        @pl.when(hi != core)
        def _():
            sent(k, SIBLING, 32)


def per_device(tokens, w_qkv, w_out, mod_shift, mod_scale, mod_gate):
    vmem = pl.BlockSpec(memory_space=pltpu.VMEM)
    result = pl.pallas_call(
        kernel,
        out_shape=jax.ShapeDtypeStruct((TOKENS, WIDTH), jnp.bfloat16),
        in_specs=[vmem] * 6,
        out_specs=vmem,
        scratch_shapes=[
            pltpu.VMEM((64, SLOT_ROWS, WIDTH), jnp.bfloat16),
            pltpu.VMEM((WIDTH, 8), jnp.float32),
            pltpu.VMEM((64, 64, TOKENS), jnp.float32),
            pltpu.VMEM((3 * HEADS, HEAD_DIM, TOKENS), jnp.bfloat16),
            pltpu.VMEM((WIDTH, TOKENS), jnp.float32),
            pltpu.VMEM((WIDTH, TOKENS), jnp.float32),
            pltpu.VMEM((WIDTH, TOKENS), jnp.bfloat16),
            pltpu.VMEM((WIDTH, TOKENS), jnp.bfloat16),
            pltpu.VMEM((2, 1024, 768), jnp.bfloat16),
            pltpu.VMEM((2, 768, 1024), jnp.bfloat16),
            pltpu.VMEM((64, 16, THIRD), jnp.bfloat16),
            pltpu.VMEM((64, 16, THIRD), jnp.bfloat16),
            pltpu.VMEM((64, 16, THIRD), jnp.bfloat16),
            pltpu.VMEM((64, 16, THIRD), jnp.bfloat16),
            pltpu.SemaphoreType.DMA((len(PIECES), 6)),
            pltpu.SemaphoreType.DMA((len(PIECES), 64)),
            pltpu.SemaphoreType.DMA((2,)),
            pltpu.SemaphoreType.DMA((2,)),
            pltpu.SemaphoreType.REGULAR((2,)),
        ],
        compiler_params=pltpu.CompilerParams(
            collective_id=0, has_side_effects=True, vmem_limit_bytes=60 * 2**20
        ),
        name="latte",
    )(
        tokens.reshape(TOKENS, WIDTH),
        jnp.transpose(w_qkv, (2, 0, 1)),
        jnp.transpose(w_out, (2, 0, 1)),
        mod_shift,
        mod_scale,
        mod_gate,
    )
    return result.reshape(tokens.shape)


def solution(mesh):
    in_specs = (
        P("dp", "seq", None, None),
        P(None, None, "seq"),
        P(None, None, "seq"),
        P(),
        P(),
        P(),
    )
    return jax.shard_map(
        per_device, mesh=mesh, in_specs=in_specs, out_specs=P("dp", "seq", None, None), check_vma=False
    )
```

```python
import functools

import jax
import jax.numpy as jnp
from jax import lax
from jax.experimental import pallas as pl
from jax.experimental.pallas import tpu as pltpu
from jax.sharding import PartitionSpec as P

HEADS = 16
HEAD_DIM = 72
WIDTH = 1152
TOKENS = 256
LOG2E = 1.4426950408889634
MESH = pl.DeviceIdType.MESH

SLOT_ROWS = 144
QKV_COLS = 54
OUT_COLS = 18
PIECES = (
    (0, 32, "z", False),
    (32, 16, "y", False),
    (48, 16, "z", True),
    (64, 16, "y", True),
    (80, 32, "z", False),
    (112, 16, "z", True),
    (128, 16, "y", True),
)
GROUPS = ((0, 1, 2, 3), (), (4, 5, 6))
ORDER = (
    32, 0, 64, 96, 33, 7, 71, 103, 1, 39, 88, 65, 24, 8, 97, 56, 120, 40, 72, 104, 6, 2, 31, 66,
    70, 34, 63, 38, 98, 25, 57, 89, 112, 16, 102, 95, 47, 79, 80, 73, 41, 48, 15, 5, 3, 127, 121, 111,
    30, 67, 14, 10, 26, 105, 37, 9, 69, 35, 94, 78, 23, 58, 62, 101, 42, 99, 46, 49, 90, 74, 122, 55,
    126, 87, 119, 128, 160, 59, 110, 4, 81, 106, 192, 113, 13, 68, 11, 17, 36, 22, 50, 29, 43, 123, 77, 18,
    27, 91, 135, 60, 100, 129, 152, 45, 136, 167, 75, 161, 86, 54, 184, 107, 168, 114, 61, 199, 93, 193, 82, 51,
    216, 28, 118, 12, 200, 109, 134, 130, 125, 159, 21, 166, 53, 115, 76, 162, 153, 143, 19, 44, 124, 198, 92, 194,
    137, 117, 223, 83, 20, 217, 144, 85, 191, 133, 131, 52, 108, 207, 84, 201, 116, 185, 176, 175, 169, 208, 158, 132,
    165, 142, 163, 154, 197, 138, 195, 151, 222, 218, 206, 202, 215, 209, 164, 190, 145, 141, 196, 186, 157, 139, 221, 219,
    155, 174, 205, 203, 170, 183, 210, 214, 156, 140, 220, 177, 150, 204, 211, 146, 213, 189, 149, 173, 187, 147, 171, 212,
    148, 188, 172, 182, 178, 181, 179, 180,
)
UP_Y, DOWN_Y, UP_Z, DOWN_Z, SIBLING, OPPOSITE = range(6)
QKV_WINDOW = ((0, 0), (80, 10))
OUT_WINDOW = ((48, 6), (64, 8))


def normalise(values, shift, scale):
    mean = jnp.mean(values, axis=0, keepdims=True)
    centred = values - mean
    spread = jnp.mean(centred * centred, axis=0, keepdims=True)
    return (centred * lax.rsqrt(spread + 1e-06) * scale + shift).astype(jnp.bfloat16)


def kernel(
    x_ref, wqkv_ref, wout_ref, shift_ref, scale_ref, gate_ref, o_ref,
    slots, mod, qkv, heads, mixed, xt, nt, ft, sel_out, sel_in,
    tail, *rest_refs,
):
    bufs_a, bufs_b = rest_refs[:6], rest_refs[6:12]
    ring_send, ring_recv, a2a_send, a2a_recv, tail_sem, entered = rest_refs[12:]
    dp = lax.axis_index("dp")
    seq = lax.axis_index("seq")
    core, xlo = dp % 2, dp // 2
    hi, z, y = seq // 32, (seq // 4) % 8, seq % 4
    other = 1 - core

    def chip(yy, zz):
        return (dp, 32 * hi + 4 * ((zz + 8) % 8) + (yy + 4) % 4)

    sibling = (2 * xlo + other, seq)
    opposite = (2 * (1 - xlo) + core, 32 * (1 - hi) + 4 * z + y)
    beside = (2 * (1 - xlo) + core, seq)
    devices = (chip(y + 1, z), chip(y - 1, z), chip(y, z + 1), chip(y, z - 1), sibling, opposite)

    barrier = pltpu.get_barrier_semaphore()

    for device in (*devices, beside):
        pl.semaphore_signal(barrier, inc=1, device_id=device, device_id_type=MESH)

    columns = wqkv_ref[...].astype(jnp.float32)
    outs = wout_ref[...].astype(jnp.float32)
    rows = jnp.concatenate([columns[:, 0], outs[:, 0], outs[:, 1], columns[:, 1]], axis=0).astype(jnp.bfloat16)
    mine = 32 * hi + 4 * z + y
    slots[mine] = rows

    pl.semaphore_wait(barrier, 7)

    def part(slot, k):
        return slots.at[slot, pl.ds(PIECES[k][0], PIECES[k][1])]

    def push(slot, k, way):
        pltpu.make_async_remote_copy(
            src_ref=part(slot, k), dst_ref=part(slot, k),
            send_sem=ring_send.at[k, way], recv_sem=ring_recv.at[k, slot],
            device_id=devices[way], device_id_type=MESH,
        ).start()

    def arrive(slot, k):
        pltpu.make_async_remote_copy(
            src_ref=part(slot, k), dst_ref=part(slot, k),
            send_sem=ring_send.at[k, 0], recv_sem=ring_recv.at[k, slot],
            device_id=sibling, device_id_type=MESH,
        ).wait_recv()

    def routes(k, dy, dz):
        ways = []
        if PIECES[k][2] == "z":
            if dy == 0:
                ways += {0: [UP_Z, DOWN_Z], 3: [DOWN_Z] * (k % 2), 4: [], 5: [UP_Z] * (1 - k % 2)}.get(
                    dz, [DOWN_Z] if dz < 4 else [UP_Z]
                )
                ways += [UP_Y, DOWN_Y]
            elif dy != 2 and (dz + k) % 2 == dy // 2:
                ways += [DOWN_Y if dy == 1 else UP_Y]
        else:
            if dz == 0:
                ways += [UP_Z, DOWN_Z]
                if dy == 0:
                    ways += [UP_Y, DOWN_Y]
                elif dy != 2 and k % 2 == dy // 2:
                    ways += [DOWN_Y if dy == 1 else UP_Y]
            elif dz in (3, 5):
                if (dy + k) % 2 == dz // 4:
                    ways += [DOWN_Z if dz == 3 else UP_Z]
            elif dz != 4:
                ways += [DOWN_Z if dz < 4 else UP_Z]
        return ways

    def block_of(half, dy, dz):
        return 32 * half + 4 * lax.rem(z + dz, 8) + lax.rem(y + dy, 4)

    def event(k, dy, dz):
        slot = block_of(core, dy, dz)
        last = PIECES[k][3]
        start = dy == 0 and dz == 0

        def onward():
            for way in routes(k, dy, dz):
                push(slot, k, way)

        if start:

            @pl.when(hi != core)
            def _():
                arrive(slot, k)

            @pl.when(hi == core)
            def _():
                push(slot, k, OPPOSITE)
                if last:
                    onward()

            @pl.when(hi != core)
            def _():
                push(slot, k, SIBLING)

        else:
            arrive(slot, k)
            if last:

                @pl.when(hi == core)
                def _():
                    onward()
                    push(slot, k, OPPOSITE)

            push(slot, k, SIBLING)
        if not last:
            onward()

    def course(k):
        return [(k, dy, dz) for dy in range(4) for dz in range(8)]

    def run(events):
        for e in events:
            event(*e)

    def from_sibling(ks, dy, dz):
        slot = block_of(other, dy, dz)

        def taken():
            for k in ks:
                arrive(slot, k)

        if dy == 0 and dz == 0:
            pl.when(hi == core)(taken)
        else:
            taken()

    def all_from_sibling(ks):
        for dy in range(4):
            for dz in range(8):
                from_sibling(ks, dy, dz)

    order = [(e // 32, e // 8 % 4, e % 8) for e in ORDER]
    end_a = 1 + max(i for i, e in enumerate(order) if e[0] in GROUPS[0])
    run(order[:4])

    def prepare():
        six = jnp.concatenate([shift_ref[...], scale_ref[...], gate_ref[...], gate_ref[...]], axis=0)
        mod[...] = six.T
        xt[...] = x_ref[...].astype(jnp.float32).T
        nt[...] = normalise(xt[...], mod[:, 0:1], mod[:, 2:3])

    def token_at(by_frame, s, p):
        return 64 * p + s if by_frame else 4 * s + p

    def permutation(rows, cols):
        return jnp.where(rows == cols, 1.0, 0.0).astype(jnp.bfloat16)

    def make_sel_out(by_frame, q):
        row = lax.broadcasted_iota(jnp.int32, (256, 1), 0) + 256 * q
        want = 256 * ((row >> 2) & 3) + token_at(by_frame, row >> 4, row & 3)
        sel_out[by_frame, 256 * q : 256 * (q + 1)] = permutation(
            want, lax.broadcasted_iota(jnp.int32, (256, 1024), 1)
        )

    def make_sel_in(by_frame, q):
        col = lax.broadcasted_iota(jnp.int32, (1, 1024), 1)
        want = 256 * ((col >> 2) & 3) + token_at(by_frame, col >> 4, col & 3)
        sel_in[by_frame, 256 * q : 256 * (q + 1)] = permutation(
            lax.broadcasted_iota(jnp.int32, (256, 1024), 0) + 256 * q, want
        )

    def make_tail():
        row = lax.broadcasted_iota(jnp.int32, (256, 1), 0)
        col = lax.broadcasted_iota(jnp.int32, (1, 256), 1)
        rows = lax.broadcasted_iota(jnp.int32, (256, 256), 0)
        cols = lax.broadcasted_iota(jnp.int32, (256, 256), 1)
        for by_frame in (0, 1):
            tail[by_frame] = permutation(token_at(by_frame, row >> 2, row & 3), cols)
            sender = 4 * ((col >> 2) & 15) + (col >> 6)
            tail[2 + by_frame] = permutation(rows, token_at(by_frame, sender, col & 3))
        tail[4] = permutation(16 * ((row >> 2) & 15) + 4 * (row >> 6) + (row & 3), cols)

    def pack_and_send(bufs, by_frame):
        send_ref, recv_ref, line_out, line_in, _, _ = bufs
        line = seq // 4
        got = lax.dot_general(
            tail[by_frame], ft[1024:], (((1,), (1,)), ((), ())), preferred_element_type=jnp.float32
        )
        line_out[...] = got.astype(jnp.bfloat16).reshape(16, 16, 128)

        def along(k, _):
            to = lax.rem(line + k, 16)
            pltpu.make_async_remote_copy(
                src_ref=line_out.at[to], dst_ref=line_in.at[line],
                send_sem=tail_sem.at[0, by_frame], recv_sem=tail_sem.at[1, by_frame],
                device_id=(dp, 4 * to + y), device_id_type=MESH,
            ).start()
            return 0

        lax.fori_loop(1, 16, along, 0)
        line_in[line] = line_out[line]
        flat = jnp.concatenate([ft[256 * t : 256 * (t + 1)] for t in range(4)], axis=1)

        def quarter(c, _):
            q = lax.rem(seq // 16 + 1 + c, 4)
            packed = lax.dot_general(
                sel_out[by_frame, pl.ds(pl.multiple_of(256 * q, 256), 256)], flat,
                (((1,), (1,)), ((), ())), preferred_element_type=jnp.float32,
            )
            send_ref[pl.ds(16 * q, 16)] = packed.astype(jnp.bfloat16).reshape(16, 16, 256)

            def one(j, _):
                to = 16 * q + lax.rem(seq + j, 16)

                @pl.when(to != seq)
                def _():
                    pltpu.make_async_remote_copy(
                        src_ref=send_ref.at[to], dst_ref=recv_ref.at[seq],
                        send_sem=a2a_send.at[by_frame], recv_sem=a2a_recv.at[by_frame],
                        device_id=(dp, to), device_id_type=MESH,
                    ).start()

                return 0

            lax.fori_loop(0, 16, one, 0)
            return 0

        lax.fori_loop(0, 4, quarter, 0)
        recv_ref[seq] = send_ref[seq]

    def relay(bufs, by_frame):
        _, _, line_out, line_in, y_out, y_in = bufs
        line = seq // 4
        finish(line_out.at[pl.ds(0, 15)], line_in.at[pl.ds(0, 15)], tail_sem.at[0, by_frame], tail_sem.at[1, by_frame])
        got = jnp.dot(tail[4], line_in[...].reshape(256, 128), preferred_element_type=jnp.float32)
        y_out[...] = got.astype(jnp.bfloat16).reshape(4, 64, 128)
        for k in range(1, 4):
            to = lax.rem(y + k, 4)
            pltpu.make_async_remote_copy(
                src_ref=y_out.at[to], dst_ref=y_in.at[y],
                send_sem=tail_sem.at[2, by_frame], recv_sem=tail_sem.at[3, by_frame],
                device_id=(dp, 4 * line + to), device_id_type=MESH,
            ).start()
        y_in[y] = y_out[y]

    def finish(src, dst, send, recv):
        done = pltpu.make_async_remote_copy(
            src_ref=src, dst_ref=dst, send_sem=send, recv_sem=recv, device_id=sibling, device_id_type=MESH
        )
        done.wait_send()
        done.wait_recv()

    def exchanged(bufs, by_frame):
        send_ref, recv_ref, _, _, y_out, y_in = bufs
        finish(y_out.at[pl.ds(0, 3)], y_in.at[pl.ds(0, 3)], tail_sem.at[2, by_frame], tail_sem.at[3, by_frame])
        finish(send_ref.at[pl.ds(0, 63)], recv_ref.at[pl.ds(0, 63)], a2a_send.at[by_frame], a2a_recv.at[by_frame])

    def unpack(bufs, by_frame):
        main = jnp.dot(
            sel_in[by_frame], bufs[1][...].reshape(1024, 256), preferred_element_type=jnp.float32
        )
        last = jnp.dot(tail[2 + by_frame], bufs[5][...].reshape(256, 128), preferred_element_type=jnp.float32)
        return [main[256 * t : 256 * (t + 1)] for t in range(4)] + [last]

    def project_slots(layer, slot_list):
        first = QKV_WINDOW[layer][0]
        block = jnp.concatenate([slots[j, pl.ds(first, 64)] for j in slot_list], axis=0)
        got = jnp.dot(block, nt[...], preferred_element_type=jnp.float32)
        for n, j in enumerate(slot_list):
            qkv[j] = got[64 * n : 64 * (n + 1)]

    def project_qkv(layer):
        def one(g, _):
            project_slots(layer, [8 * g + j for j in range(8)])
            return 0

        lax.fori_loop(0, 8, one, 0)

    def split_heads(layer, lo, hi_):
        offset = QKV_WINDOW[layer][1]

        def split(g, _):
            four = [qkv[4 * g + j, offset : offset + QKV_COLS] for j in range(4)]
            units = (
                jnp.concatenate([four[0], four[1][:18]], axis=0),
                jnp.concatenate([four[1][18:], four[2][:36]], axis=0),
                jnp.concatenate([four[2][36:], four[3]], axis=0),
            )
            for j, unit in enumerate(units):
                at = 3 * g + j
                factor = jnp.where(at < HEADS, HEAD_DIM**-0.5 * LOG2E, 1.0).astype(jnp.float32)
                heads[at] = (unit * factor).astype(jnp.bfloat16)
            return 0

        lax.fori_loop(lo, hi_, split, 0)

    def scores_of(h):
        return lax.dot_general(
            heads[HEADS + h], heads[h], (((0,), (0,)), ((), ())), preferred_element_type=jnp.float32
        )

    def mix(h, weights, total):
        got = jnp.dot(heads[2 * HEADS + h], weights, preferred_element_type=jnp.float32)
        mixed[pl.ds(pl.multiple_of(HEAD_DIM * h, 8), HEAD_DIM)] = got / total

    def attend_space(h):
        scores = scores_of(h)
        weights = jnp.exp2(scores - jnp.max(scores, axis=0, keepdims=True))
        total = jnp.sum(weights, axis=0, keepdims=True)
        mix(h, weights.astype(jnp.bfloat16), total)

    def attend_time(h):
        scores = scores_of(h)
        low = lax.broadcasted_iota(jnp.int32, (64, 128), 1) < 64
        near = jnp.concatenate(
            [
                jnp.where(low, scores[0:64, 0:128], scores[64:128, 0:128]),
                jnp.where(low, scores[128:192, 128:256], scores[192:256, 128:256]),
            ],
            axis=1,
        )
        weights = jnp.exp2(near - jnp.max(near, axis=0, keepdims=True))
        total = jnp.sum(weights, axis=0, keepdims=True)
        column = lax.broadcasted_iota(jnp.int32, (64, TOKENS), 1) // 64
        spread = jnp.concatenate([jnp.where(column == p, weights, 0.0) for p in range(4)], axis=0)
        mix(h, spread.astype(jnp.bfloat16), total)

    def project_out(layer, lo, hi_):
        first, offset = OUT_WINDOW[layer]

        def one(g, _):
            block = slots[pl.ds(8 * g, 8), pl.ds(first, 32)].reshape(256, WIDTH)
            got = jnp.dot(block, nt[...], preferred_element_type=jnp.float32).reshape(8, 32, TOKENS)
            got = jnp.concatenate([got[j, offset : offset + OUT_COLS] for j in range(8)], axis=0)
            at = pl.ds(pl.multiple_of(144 * g, 16), 144)
            ft[at] = (xt[at] + mod[at, 4 + layer : 5 + layer] * got).astype(jnp.bfloat16)
            return 0

        lax.fori_loop(lo, hi_, one, 0)

    def over_heads(attend, lo, hi_, step=2):
        def one(n, _):
            for j in range(step):
                attend(lo + step * n + j)
            return 0

        lax.fori_loop(0, (hi_ - lo) // step, one, 0)

    done = {}
    for i, (k, dy, dz) in enumerate(order[:end_a]):
        if k in GROUPS[0]:
            done[dy, dz] = i
    blocks = sorted(done, key=done.get)
    batches = [blocks[n : n + 4] for n in range(0, 32, 4)]
    after = {}
    tasks = [make_tail]
    for by_frame in (0, 1):
        tasks += [functools.partial(make_sel_out, by_frame, q) for q in range(4)]
        tasks += [functools.partial(make_sel_in, 1 - by_frame, q) for q in range(4)]
    for n, task in enumerate([prepare] + tasks):
        after.setdefault(6 + 4 * n, []).append(task)

    def batch(n):
        ready = [block_of(core, dy, dz) for dy, dz in batches[n]] if n < 8 else []
        if n > 0:
            for dy, dz in batches[n - 1]:
                from_sibling(GROUPS[0], dy, dz)
                ready.append(block_of(other, dy, dz))
        project_slots(0, ready)

    for n in range(8):
        after.setdefault(max(done[block] for block in batches[n]), []).append(functools.partial(batch, n))
    for i in range(4, end_a):
        run(order[i : i + 1])
        for task in after.get(i, []):
            task()
    batch(8)

    def tell(n, device):
        pl.semaphore_signal(entered.at[n], inc=1, device_id=device, device_id_type=MESH)

    tell(0, opposite)

    rest = order[end_a:]

    def more(count):
        run(rest[:count])
        del rest[:count]

    for q in range(4):
        split_heads(0, 4 * q, 4 * q + 4)
        more(2)
    for q in range(8):
        over_heads(attend_space, 2 * q, 2 * q + 2)
        more(2)
    pl.semaphore_wait(entered.at[0], 1)
    tell(1, beside)
    if GROUPS[1]:
        more(1 + max([i for i, e in enumerate(rest) if e[0] in GROUPS[1]], default=-1))
        all_from_sibling(GROUPS[1])
    nt[...] = mixed[...].astype(jnp.bfloat16)
    for q in range(4):
        project_out(0, 2 * q, 2 * q + 2)
        more(2)
    pl.semaphore_wait(entered.at[1], 1)
    pack_and_send(bufs_a, 0)
    more(len(rest) // 2)
    relay(bufs_a, 0)
    more(len(rest))
    all_from_sibling(GROUPS[2])
    exchanged(bufs_a, 0)

    for t, got in enumerate(unpack(bufs_a, 1)):
        xt[256 * t : 256 * t + got.shape[1]] = got.T
    nt[...] = normalise(xt[...], mod[:, 1:2], mod[:, 3:4])
    project_qkv(1)
    split_heads(1, 0, 16)
    over_heads(attend_time, 0, HEADS, 4)
    nt[...] = mixed[...].astype(jnp.bfloat16)
    project_out(1, 0, 8)
    pack_and_send(bufs_b, 1)
    relay(bufs_b, 1)
    exchanged(bufs_b, 1)
    for t, got in enumerate(unpack(bufs_b, 0)):
        o_ref[:, 256 * t : 256 * t + got.shape[1]] = got.astype(jnp.bfloat16)

    def sent(k, way, count):
        rows = pl.ds(PIECES[k][0], PIECES[k][1])
        pltpu.make_async_remote_copy(
            src_ref=slots.at[pl.ds(0, count), rows], dst_ref=slots.at[pl.ds(0, count), rows],
            send_sem=ring_send.at[k, way], recv_sem=ring_recv.at[k, 0],
            device_id=sibling, device_id_type=MESH,
        ).wait_send()

    for k, piece in enumerate(PIECES):
        ways = [way for e in course(k) for way in routes(*e)]

        def plane_sent():
            for way in (UP_Y, DOWN_Y, UP_Z, DOWN_Z):
                sent(k, way, ways.count(way))

        if not piece[3]:
            plane_sent()

        @pl.when(hi == core)
        def _():
            if piece[3]:
                plane_sent()
            sent(k, OPPOSITE, 32 if piece[3] else 1)
            sent(k, SIBLING, 31)

        @pl.when(hi != core)
        def _():
            sent(k, SIBLING, 32)


def per_device(tokens, w_qkv, w_out, mod_shift, mod_scale, mod_gate):
    vmem = pl.BlockSpec(memory_space=pltpu.VMEM)
    exchange_buffers = [
        pltpu.VMEM(shape, jnp.bfloat16)
        for shape in ((64, 16, 256), (64, 16, 256), (16, 16, 128), (16, 16, 128), (4, 64, 128), (4, 64, 128))
    ]
    result = pl.pallas_call(
        kernel,
        out_shape=jax.ShapeDtypeStruct((TOKENS, WIDTH), jnp.bfloat16),
        in_specs=[vmem] * 6,
        out_specs=vmem,
        scratch_shapes=[
            pltpu.VMEM((64, SLOT_ROWS, WIDTH), jnp.bfloat16),
            pltpu.VMEM((WIDTH, 8), jnp.float32),
            pltpu.VMEM((64, 64, TOKENS), jnp.float32),
            pltpu.VMEM((3 * HEADS, HEAD_DIM, TOKENS), jnp.bfloat16),
            pltpu.VMEM((WIDTH, TOKENS), jnp.float32),
            pltpu.VMEM((WIDTH, TOKENS), jnp.float32),
            pltpu.VMEM((WIDTH, TOKENS), jnp.bfloat16),
            pltpu.VMEM((WIDTH, TOKENS), jnp.bfloat16),
            pltpu.VMEM((2, 1024, 1024), jnp.bfloat16),
            pltpu.VMEM((2, 1024, 1024), jnp.bfloat16),
            pltpu.VMEM((5, 256, 256), jnp.bfloat16),
            *exchange_buffers,
            *exchange_buffers,
            pltpu.SemaphoreType.DMA((len(PIECES), 6)),
            pltpu.SemaphoreType.DMA((len(PIECES), 64)),
            pltpu.SemaphoreType.DMA((2,)),
            pltpu.SemaphoreType.DMA((2,)),
            pltpu.SemaphoreType.DMA((4, 2)),
            pltpu.SemaphoreType.REGULAR((2,)),
        ],
        compiler_params=pltpu.CompilerParams(
            collective_id=0, has_side_effects=True, vmem_limit_bytes=60 * 2**20
        ),
        name="latte",
    )(
        tokens.reshape(TOKENS, WIDTH),
        jnp.transpose(w_qkv, (2, 0, 1)),
        jnp.transpose(w_out, (2, 0, 1)),
        mod_shift,
        mod_scale,
        mod_gate,
    )
    return result.reshape(tokens.shape)


def solution(mesh):
    in_specs = (
        P("dp", "seq", None, None),
        P(None, None, "seq"),
        P(None, None, "seq"),
        P(),
        P(),
        P(),
    )
    return jax.shard_map(
        per_device, mesh=mesh, in_specs=in_specs, out_specs=P("dp", "seq", None, None), check_vma=False
    )
```

```python
import functools

import jax
import jax.numpy as jnp
from jax import lax
from jax.experimental import pallas as pl
from jax.experimental.pallas import tpu as pltpu
from jax.sharding import PartitionSpec as P

HEADS = 16
HEAD_DIM = 72
WIDTH = 1152
TOKENS = 256
LOG2E = 1.4426950408889634
MESH = pl.DeviceIdType.MESH

SLOT_ROWS = 144
QKV_COLS = 54
OUT_COLS = 18
PIECES = (
    (0, 32, "z", False),
    (32, 16, "y", False),
    (48, 16, "z", True),
    (64, 16, "y", True),
    (80, 32, "z", False),
    (112, 16, "z", True),
    (128, 16, "y", True),
)
GROUPS = ((0, 1, 2, 3), (), (4, 5, 6))
ORDER = (
    32, 0, 64, 96, 33, 7, 71, 103, 1, 39, 88, 65, 24, 8, 97, 56, 120, 40, 72, 104, 6, 2, 31, 66,
    70, 34, 63, 38, 98, 25, 57, 89, 112, 16, 102, 95, 47, 79, 80, 73, 41, 48, 15, 5, 3, 127, 121, 111,
    30, 67, 14, 10, 26, 105, 37, 9, 69, 35, 94, 78, 23, 58, 62, 101, 42, 99, 46, 49, 90, 74, 122, 55,
    126, 87, 119, 128, 160, 59, 110, 4, 81, 106, 192, 113, 13, 68, 11, 17, 36, 22, 50, 29, 43, 123, 77, 18,
    27, 91, 135, 60, 100, 129, 152, 45, 136, 167, 75, 161, 86, 54, 184, 107, 168, 114, 61, 199, 93, 193, 82, 51,
    216, 28, 118, 12, 200, 109, 134, 130, 125, 159, 21, 166, 53, 115, 76, 162, 153, 143, 19, 44, 124, 198, 92, 194,
    137, 117, 223, 83, 20, 217, 144, 85, 191, 133, 131, 52, 108, 207, 84, 201, 116, 185, 176, 175, 169, 208, 158, 132,
    165, 142, 163, 154, 197, 138, 195, 151, 222, 218, 206, 202, 215, 209, 164, 190, 145, 141, 196, 186, 157, 139, 221, 219,
    155, 174, 205, 203, 170, 183, 210, 214, 156, 140, 220, 177, 150, 204, 211, 146, 213, 189, 149, 173, 187, 147, 171, 212,
    148, 188, 172, 182, 178, 181, 179, 180,
)
UP_Y, DOWN_Y, UP_Z, DOWN_Z, SIBLING, OPPOSITE = range(6)
QKV_WINDOW = ((0, 0), (80, 10))
OUT_WINDOW = ((48, 6), (64, 8))


def normalise(values, shift, scale):
    mean = jnp.mean(values, axis=0, keepdims=True)
    centred = values - mean
    spread = jnp.mean(centred * centred, axis=0, keepdims=True)
    return (centred * lax.rsqrt(spread + 1e-06) * scale + shift).astype(jnp.bfloat16)


def kernel(
    x_ref, wqkv_ref, wout_ref, shift_ref, scale_ref, gate_ref, o_ref,
    slots, mod, qkv, heads, mixed, xt, nt, ft, sel_out, sel_in,
    tail, *rest_refs,
):
    bufs_a, bufs_b = rest_refs[:6], rest_refs[6:12]
    ring_send, ring_recv, a2a_send, a2a_recv, tail_sem, entered = rest_refs[12:]
    dp = lax.axis_index("dp")
    seq = lax.axis_index("seq")
    core, xlo = dp % 2, dp // 2
    hi, z, y = seq // 32, (seq // 4) % 8, seq % 4
    other = 1 - core

    def chip(yy, zz):
        return (dp, 32 * hi + 4 * ((zz + 8) % 8) + (yy + 4) % 4)

    sibling = (2 * xlo + other, seq)
    opposite = (2 * (1 - xlo) + core, 32 * (1 - hi) + 4 * z + y)
    beside = (2 * (1 - xlo) + core, seq)
    devices = (chip(y + 1, z), chip(y - 1, z), chip(y, z + 1), chip(y, z - 1), sibling, opposite)

    barrier = pltpu.get_barrier_semaphore()

    for device in (*devices, beside):
        pl.semaphore_signal(barrier, inc=1, device_id=device, device_id_type=MESH)

    columns = wqkv_ref[...].astype(jnp.float32)
    outs = wout_ref[...].astype(jnp.float32)
    rows = jnp.concatenate([columns[:, 0], outs[:, 0], outs[:, 1], columns[:, 1]], axis=0).astype(jnp.bfloat16)
    mine = 32 * hi + 4 * z + y
    slots[mine] = rows

    pl.semaphore_wait(barrier, 7)

    def part(slot, k):
        return slots.at[slot, pl.ds(PIECES[k][0], PIECES[k][1])]

    def push(slot, k, way):
        pltpu.make_async_remote_copy(
            src_ref=part(slot, k), dst_ref=part(slot, k),
            send_sem=ring_send.at[k, way], recv_sem=ring_recv.at[k, slot],
            device_id=devices[way], device_id_type=MESH,
        ).start()

    def arrive(slot, k):
        pltpu.make_async_remote_copy(
            src_ref=part(slot, k), dst_ref=part(slot, k),
            send_sem=ring_send.at[k, 0], recv_sem=ring_recv.at[k, slot],
            device_id=sibling, device_id_type=MESH,
        ).wait_recv()

    def routes(k, dy, dz):
        ways = []
        if PIECES[k][2] == "z":
            if dy == 0:
                ways += {0: [UP_Z, DOWN_Z], 3: [DOWN_Z] * (k % 2), 4: [], 5: [UP_Z] * (1 - k % 2)}.get(
                    dz, [DOWN_Z] if dz < 4 else [UP_Z]
                )
                ways += [UP_Y, DOWN_Y]
            elif dy != 2 and (dz + k) % 2 == dy // 2:
                ways += [DOWN_Y if dy == 1 else UP_Y]
        else:
            if dz == 0:
                ways += [UP_Z, DOWN_Z]
                if dy == 0:
                    ways += [UP_Y, DOWN_Y]
                elif dy != 2 and k % 2 == dy // 2:
                    ways += [DOWN_Y if dy == 1 else UP_Y]
            elif dz in (3, 5):
                if (dy + k) % 2 == dz // 4:
                    ways += [DOWN_Z if dz == 3 else UP_Z]
            elif dz != 4:
                ways += [DOWN_Z if dz < 4 else UP_Z]
        return ways

    def block_of(half, dy, dz):
        return 32 * half + 4 * lax.rem(z + dz, 8) + lax.rem(y + dy, 4)

    def event(k, dy, dz):
        slot = block_of(core, dy, dz)
        last = PIECES[k][3]
        start = dy == 0 and dz == 0

        def onward():
            for way in routes(k, dy, dz):
                push(slot, k, way)

        if start:

            @pl.when(hi != core)
            def _():
                arrive(slot, k)

            @pl.when(hi == core)
            def _():
                push(slot, k, OPPOSITE)
                if last:
                    onward()

            @pl.when(hi != core)
            def _():
                push(slot, k, SIBLING)

        else:
            arrive(slot, k)
            if last:

                @pl.when(hi == core)
                def _():
                    onward()
                    push(slot, k, OPPOSITE)

            push(slot, k, SIBLING)
        if not last:
            onward()

    def course(k):
        return [(k, dy, dz) for dy in range(4) for dz in range(8)]

    def run(events):
        for e in events:
            event(*e)

    def from_sibling(ks, dy, dz):
        slot = block_of(other, dy, dz)

        def taken():
            for k in ks:
                arrive(slot, k)

        if dy == 0 and dz == 0:
            pl.when(hi == core)(taken)
        else:
            taken()

    def all_from_sibling(ks):
        for dy in range(4):
            for dz in range(8):
                from_sibling(ks, dy, dz)

    order = [(e // 32, e // 8 % 4, e % 8) for e in ORDER]
    end_a = 1 + max(i for i, e in enumerate(order) if e[0] in GROUPS[0])
    run(order[:4])

    def prepare():
        six = jnp.concatenate([shift_ref[...], scale_ref[...], gate_ref[...], gate_ref[...]], axis=0)
        mod[...] = six.T
        xt[...] = x_ref[...].astype(jnp.float32).T
        nt[...] = normalise(xt[...], mod[:, 0:1], mod[:, 2:3])

    def token_at(by_frame, s, p):
        return 64 * p + s if by_frame else 4 * s + p

    def permutation(rows, cols):
        return jnp.where(rows == cols, 1.0, 0.0).astype(jnp.bfloat16)

    def make_sel_out(by_frame, q):
        row = lax.broadcasted_iota(jnp.int32, (256, 1), 0) + 256 * q
        want = 256 * ((row >> 2) & 3) + token_at(by_frame, row >> 4, row & 3)
        sel_out[by_frame, 256 * q : 256 * (q + 1)] = permutation(
            want, lax.broadcasted_iota(jnp.int32, (256, 1024), 1)
        )

    def make_sel_in(by_frame, q):
        col = lax.broadcasted_iota(jnp.int32, (1, 1024), 1)
        want = 256 * ((col >> 2) & 3) + token_at(by_frame, col >> 4, col & 3)
        sel_in[by_frame, 256 * q : 256 * (q + 1)] = permutation(
            lax.broadcasted_iota(jnp.int32, (256, 1024), 0) + 256 * q, want
        )

    def make_tail():
        row = lax.broadcasted_iota(jnp.int32, (256, 1), 0)
        col = lax.broadcasted_iota(jnp.int32, (1, 256), 1)
        rows = lax.broadcasted_iota(jnp.int32, (256, 256), 0)
        cols = lax.broadcasted_iota(jnp.int32, (256, 256), 1)
        for by_frame in (0, 1):
            tail[by_frame] = permutation(token_at(by_frame, row >> 2, row & 3), cols)
            sender = 4 * ((col >> 2) & 15) + (col >> 6)
            tail[2 + by_frame] = permutation(rows, token_at(by_frame, sender, col & 3))
        tail[4] = permutation(16 * ((row >> 2) & 15) + 4 * (row >> 6) + (row & 3), cols)

    def pack_and_send(bufs, by_frame, between=None):
        send_ref, recv_ref, line_out, line_in, _, _ = bufs
        line = seq // 4
        got = lax.dot_general(
            tail[by_frame], ft[1024:], (((1,), (1,)), ((), ())), preferred_element_type=jnp.float32
        )
        line_out[...] = got.astype(jnp.bfloat16).reshape(16, 16, 128)

        def along(k, _):
            to = lax.rem(line + k, 16)
            pltpu.make_async_remote_copy(
                src_ref=line_out.at[to], dst_ref=line_in.at[line],
                send_sem=tail_sem.at[0, by_frame], recv_sem=tail_sem.at[1, by_frame],
                device_id=(dp, 4 * to + y), device_id_type=MESH,
            ).start()
            return 0

        lax.fori_loop(1, 16, along, 0)
        line_in[line] = line_out[line]
        flat = jnp.concatenate([ft[256 * t : 256 * (t + 1)] for t in range(4)], axis=1)

        def quarter(c, _):
            q = lax.rem(seq // 16 + 1 + c, 4)
            packed = lax.dot_general(
                sel_out[by_frame, pl.ds(pl.multiple_of(256 * q, 256), 256)], flat,
                (((1,), (1,)), ((), ())), preferred_element_type=jnp.float32,
            )
            send_ref[pl.ds(16 * q, 16)] = packed.astype(jnp.bfloat16).reshape(16, 16, 256)

            def one(j, _):
                to = 16 * q + lax.rem(seq + j, 16)

                @pl.when(to != seq)
                def _():
                    pltpu.make_async_remote_copy(
                        src_ref=send_ref.at[to], dst_ref=recv_ref.at[seq],
                        send_sem=a2a_send.at[by_frame], recv_sem=a2a_recv.at[by_frame],
                        device_id=(dp, to), device_id_type=MESH,
                    ).start()

                return 0

            lax.fori_loop(0, 16, one, 0)
            return 0

        if between is None:
            lax.fori_loop(0, 4, quarter, 0)
        else:
            for c in range(4):
                between()
                quarter(c, 0)
        recv_ref[seq] = send_ref[seq]

    def relay(bufs, by_frame):
        _, _, line_out, line_in, y_out, y_in = bufs
        line = seq // 4
        finish(line_out.at[pl.ds(0, 15)], line_in.at[pl.ds(0, 15)], tail_sem.at[0, by_frame], tail_sem.at[1, by_frame])
        got = jnp.dot(tail[4], line_in[...].reshape(256, 128), preferred_element_type=jnp.float32)
        y_out[...] = got.astype(jnp.bfloat16).reshape(4, 64, 128)
        for k in range(1, 4):
            to = lax.rem(y + k, 4)
            pltpu.make_async_remote_copy(
                src_ref=y_out.at[to], dst_ref=y_in.at[y],
                send_sem=tail_sem.at[2, by_frame], recv_sem=tail_sem.at[3, by_frame],
                device_id=(dp, 4 * line + to), device_id_type=MESH,
            ).start()
        y_in[y] = y_out[y]

    def finish(src, dst, send, recv):
        done = pltpu.make_async_remote_copy(
            src_ref=src, dst_ref=dst, send_sem=send, recv_sem=recv, device_id=sibling, device_id_type=MESH
        )
        done.wait_send()
        done.wait_recv()

    def exchanged(bufs, by_frame):
        send_ref, recv_ref, _, _, y_out, y_in = bufs
        finish(y_out.at[pl.ds(0, 3)], y_in.at[pl.ds(0, 3)], tail_sem.at[2, by_frame], tail_sem.at[3, by_frame])
        finish(send_ref.at[pl.ds(0, 63)], recv_ref.at[pl.ds(0, 63)], a2a_send.at[by_frame], a2a_recv.at[by_frame])

    def unpack(bufs, by_frame):
        main = jnp.dot(
            sel_in[by_frame], bufs[1][...].reshape(1024, 256), preferred_element_type=jnp.float32
        )
        last = jnp.dot(tail[2 + by_frame], bufs[5][...].reshape(256, 128), preferred_element_type=jnp.float32)
        return [main[256 * t : 256 * (t + 1)] for t in range(4)] + [last]

    def project_slots(layer, slot_list):
        first = QKV_WINDOW[layer][0]
        block = jnp.concatenate([slots[j, pl.ds(first, 64)] for j in slot_list], axis=0)
        got = jnp.dot(block, nt[...], preferred_element_type=jnp.float32)
        for n, j in enumerate(slot_list):
            qkv[j] = got[64 * n : 64 * (n + 1)]

    def project_qkv(layer):
        def one(g, _):
            project_slots(layer, [8 * g + j for j in range(8)])
            return 0

        lax.fori_loop(0, 8, one, 0)

    def split_heads(layer, lo, hi_):
        offset = QKV_WINDOW[layer][1]

        def split(g, _):
            four = [qkv[4 * g + j, offset : offset + QKV_COLS] for j in range(4)]
            units = (
                jnp.concatenate([four[0], four[1][:18]], axis=0),
                jnp.concatenate([four[1][18:], four[2][:36]], axis=0),
                jnp.concatenate([four[2][36:], four[3]], axis=0),
            )
            for j, unit in enumerate(units):
                at = 3 * g + j
                factor = jnp.where(at < HEADS, HEAD_DIM**-0.5 * LOG2E, 1.0).astype(jnp.float32)
                heads[at] = (unit * factor).astype(jnp.bfloat16)
            return 0

        lax.fori_loop(lo, hi_, split, 0)

    def scores_of(h):
        return lax.dot_general(
            heads[HEADS + h], heads[h], (((0,), (0,)), ((), ())), preferred_element_type=jnp.float32
        )

    def mix(h, weights, total):
        got = jnp.dot(heads[2 * HEADS + h], weights, preferred_element_type=jnp.float32)
        mixed[pl.ds(pl.multiple_of(HEAD_DIM * h, 8), HEAD_DIM)] = got / total

    def attend_space(h):
        scores = scores_of(h)
        weights = jnp.exp2(scores - jnp.max(scores, axis=0, keepdims=True))
        total = jnp.sum(weights, axis=0, keepdims=True)
        mix(h, weights.astype(jnp.bfloat16), total)

    def attend_time(h):
        scores = scores_of(h)
        low = lax.broadcasted_iota(jnp.int32, (64, 128), 1) < 64
        near = jnp.concatenate(
            [
                jnp.where(low, scores[0:64, 0:128], scores[64:128, 0:128]),
                jnp.where(low, scores[128:192, 128:256], scores[192:256, 128:256]),
            ],
            axis=1,
        )
        weights = jnp.exp2(near - jnp.max(near, axis=0, keepdims=True))
        total = jnp.sum(weights, axis=0, keepdims=True)
        column = lax.broadcasted_iota(jnp.int32, (64, TOKENS), 1) // 64
        spread = jnp.concatenate([jnp.where(column == p, weights, 0.0) for p in range(4)], axis=0)
        mix(h, spread.astype(jnp.bfloat16), total)

    def project_out(layer, lo, hi_):
        first, offset = OUT_WINDOW[layer]

        def one(g, _):
            block = slots[pl.ds(8 * g, 8), pl.ds(first, 32)].reshape(256, WIDTH)
            got = jnp.dot(block, nt[...], preferred_element_type=jnp.float32).reshape(8, 32, TOKENS)
            got = jnp.concatenate([got[j, offset : offset + OUT_COLS] for j in range(8)], axis=0)
            at = pl.ds(pl.multiple_of(144 * g, 16), 144)
            ft[at] = (xt[at] + mod[at, 4 + layer : 5 + layer] * got).astype(jnp.bfloat16)
            return 0

        lax.fori_loop(lo, hi_, one, 0)

    def over_heads(attend, lo, hi_, step=2):
        def one(n, _):
            for j in range(step):
                attend(lo + step * n + j)
            return 0

        lax.fori_loop(0, (hi_ - lo) // step, one, 0)

    done = {}
    for i, (k, dy, dz) in enumerate(order[:end_a]):
        if k in GROUPS[0]:
            done[dy, dz] = i
    blocks = sorted(done, key=done.get)
    batches = [blocks[n : n + 4] for n in range(0, 32, 4)]
    after = {}
    tasks = [make_tail]
    for by_frame in (0, 1):
        tasks += [functools.partial(make_sel_out, by_frame, q) for q in range(4)]
    tasks += [functools.partial(make_sel_in, 0, q) for q in range(4)]
    for n, task in enumerate([prepare] + tasks):
        after.setdefault(6 + 4 * n, []).append(task)

    def batch(n):
        ready = [block_of(core, dy, dz) for dy, dz in batches[n]] if n < 8 else []
        if n > 0:
            for dy, dz in batches[n - 1]:
                from_sibling(GROUPS[0], dy, dz)
                ready.append(block_of(other, dy, dz))
        project_slots(0, ready)

    for n in range(8):
        after.setdefault(max(done[block] for block in batches[n]), []).append(functools.partial(batch, n))
    for i in range(4, end_a):
        run(order[i : i + 1])
        for task in after.get(i, []):
            task()
    batch(8)

    def tell(n, device):
        pl.semaphore_signal(entered.at[n], inc=1, device_id=device, device_id_type=MESH)

    tell(0, opposite)

    rest = order[end_a:]

    def more(count):
        run(rest[:count])
        del rest[:count]

    for q in range(4):
        split_heads(0, 4 * q, 4 * q + 4)
        more(2)
    for q in range(8):
        over_heads(attend_space, 2 * q, 2 * q + 2)
        more(2)
    pl.semaphore_wait(entered.at[0], 1)
    tell(1, beside)
    if GROUPS[1]:
        more(1 + max([i for i, e in enumerate(rest) if e[0] in GROUPS[1]], default=-1))
        all_from_sibling(GROUPS[1])
    nt[...] = mixed[...].astype(jnp.bfloat16)
    for q in range(4):
        project_out(0, 2 * q, 2 * q + 2)
        more(2)
    pl.semaphore_wait(entered.at[1], 1)
    pack_and_send(bufs_a, 0, functools.partial(more, 4))
    more(len(rest) // 2)
    relay(bufs_a, 0)
    more(len(rest))
    all_from_sibling(GROUPS[2])
    exchanged(bufs_a, 0)

    got = lax.dot_general(
        bufs_a[1][...].reshape(1024, 256), sel_out[1],
        (((0,), (0,)), ((), ())), preferred_element_type=jnp.float32,
    )
    for t in range(4):
        xt[256 * t : 256 * (t + 1)] = got[:, 256 * t : 256 * (t + 1)]
    last = jnp.dot(tail[3], bufs_a[5][...].reshape(256, 128), preferred_element_type=jnp.float32)
    xt[1024:] = last.T
    nt[...] = normalise(xt[...], mod[:, 1:2], mod[:, 3:4])
    project_qkv(1)
    split_heads(1, 0, 16)
    over_heads(attend_time, 0, HEADS, 4)
    nt[...] = mixed[...].astype(jnp.bfloat16)
    project_out(1, 0, 8)
    pack_and_send(bufs_b, 1)
    relay(bufs_b, 1)
    exchanged(bufs_b, 1)
    for t, got in enumerate(unpack(bufs_b, 0)):
        o_ref[:, 256 * t : 256 * t + got.shape[1]] = got.astype(jnp.bfloat16)

    def sent(k, way, count):
        rows = pl.ds(PIECES[k][0], PIECES[k][1])
        pltpu.make_async_remote_copy(
            src_ref=slots.at[pl.ds(0, count), rows], dst_ref=slots.at[pl.ds(0, count), rows],
            send_sem=ring_send.at[k, way], recv_sem=ring_recv.at[k, 0],
            device_id=sibling, device_id_type=MESH,
        ).wait_send()

    for k, piece in enumerate(PIECES):
        ways = [way for e in course(k) for way in routes(*e)]

        def plane_sent():
            for way in (UP_Y, DOWN_Y, UP_Z, DOWN_Z):
                sent(k, way, ways.count(way))

        if not piece[3]:
            plane_sent()

        @pl.when(hi == core)
        def _():
            if piece[3]:
                plane_sent()
            sent(k, OPPOSITE, 32 if piece[3] else 1)
            sent(k, SIBLING, 31)

        @pl.when(hi != core)
        def _():
            sent(k, SIBLING, 32)


def per_device(tokens, w_qkv, w_out, mod_shift, mod_scale, mod_gate):
    vmem = pl.BlockSpec(memory_space=pltpu.VMEM)
    exchange_buffers = [
        pltpu.VMEM(shape, jnp.bfloat16)
        for shape in ((64, 16, 256), (64, 16, 256), (16, 16, 128), (16, 16, 128), (4, 64, 128), (4, 64, 128))
    ]
    result = pl.pallas_call(
        kernel,
        out_shape=jax.ShapeDtypeStruct((TOKENS, WIDTH), jnp.bfloat16),
        in_specs=[vmem] * 6,
        out_specs=vmem,
        scratch_shapes=[
            pltpu.VMEM((64, SLOT_ROWS, WIDTH), jnp.bfloat16),
            pltpu.VMEM((WIDTH, 8), jnp.float32),
            pltpu.VMEM((64, 64, TOKENS), jnp.float32),
            pltpu.VMEM((3 * HEADS, HEAD_DIM, TOKENS), jnp.bfloat16),
            pltpu.VMEM((WIDTH, TOKENS), jnp.float32),
            pltpu.VMEM((WIDTH, TOKENS), jnp.float32),
            pltpu.VMEM((WIDTH, TOKENS), jnp.bfloat16),
            pltpu.VMEM((WIDTH, TOKENS), jnp.bfloat16),
            pltpu.VMEM((2, 1024, 1024), jnp.bfloat16),
            pltpu.VMEM((1, 1024, 1024), jnp.bfloat16),
            pltpu.VMEM((5, 256, 256), jnp.bfloat16),
            *exchange_buffers,
            *exchange_buffers,
            pltpu.SemaphoreType.DMA((len(PIECES), 6)),
            pltpu.SemaphoreType.DMA((len(PIECES), 64)),
            pltpu.SemaphoreType.DMA((2,)),
            pltpu.SemaphoreType.DMA((2,)),
            pltpu.SemaphoreType.DMA((4, 2)),
            pltpu.SemaphoreType.REGULAR((2,)),
        ],
        compiler_params=pltpu.CompilerParams(
            collective_id=0, has_side_effects=True, vmem_limit_bytes=60 * 2**20
        ),
        name="latte",
    )(
        tokens.reshape(TOKENS, WIDTH),
        jnp.transpose(w_qkv, (2, 0, 1)),
        jnp.transpose(w_out, (2, 0, 1)),
        mod_shift,
        mod_scale,
        mod_gate,
    )
    return result.reshape(tokens.shape)


def solution(mesh):
    in_specs = (
        P("dp", "seq", None, None),
        P(None, None, "seq"),
        P(None, None, "seq"),
        P(),
        P(),
        P(),
    )
    return jax.shard_map(
        per_device, mesh=mesh, in_specs=in_specs, out_specs=P("dp", "seq", None, None), check_vma=False
    )
```

```python
import functools

import jax
import jax.numpy as jnp
from jax import lax
from jax.experimental import pallas as pl
from jax.experimental.pallas import tpu as pltpu
from jax.sharding import PartitionSpec as P

HEADS = 16
HEAD_DIM = 72
WIDTH = 1152
TOKENS = 256
LOG2E = 1.4426950408889634
MESH = pl.DeviceIdType.MESH

SLOT_ROWS = 144
QKV_COLS = 54
OUT_COLS = 18
PIECES = (
    (0, 32, "z", False),
    (32, 16, "y", False),
    (48, 16, "z", True),
    (64, 16, "y", True),
    (80, 32, "z", False),
    (112, 16, "z", True),
    (128, 16, "y", True),
)
GROUPS = ((0, 1, 2, 3), (), (4, 5, 6))
ORDER = (
    0, 64, 32, 96, 7, 1, 65, 33, 71, 39, 56, 40, 72, 103, 97, 120, 8, 6, 31, 104, 2, 15, 24, 88,
    38, 66, 25, 70, 34, 102, 57, 63, 95, 98, 89, 121, 73, 41, 47, 79, 9, 127, 80, 48, 111, 112, 105, 5,
    37, 14, 23, 16, 69, 35, 3, 10, 99, 67, 58, 78, 42, 101, 62, 87, 30, 46, 94, 74, 26, 17, 49, 90,
    55, 126, 122, 110, 113, 59, 128, 4, 119, 160, 106, 192, 81, 11, 43, 50, 13, 75, 29, 36, 114, 18, 86, 27,
    68, 123, 61, 135, 129, 152, 136, 167, 77, 22, 161, 100, 60, 184, 107, 54, 168, 44, 93, 199, 91, 45, 193, 125,
    51, 28, 216, 118, 12, 200, 82, 134, 130, 124, 159, 21, 115, 166, 53, 162, 153, 143, 19, 108, 76, 198, 92, 194,
    137, 117, 223, 109, 217, 144, 85, 191, 133, 131, 83, 20, 52, 207, 84, 201, 116, 185, 176, 175, 169, 208, 158, 132,
    165, 142, 163, 154, 197, 138, 195, 151, 222, 218, 206, 202, 215, 209, 164, 190, 145, 141, 196, 186, 157, 139, 221, 219,
    155, 174, 205, 203, 170, 183, 210, 214, 156, 140, 220, 177, 150, 204, 211, 146, 213, 189, 149, 173, 187, 147, 171, 212,
    148, 188, 172, 182, 178, 181, 179, 180,
)
UP_Y, DOWN_Y, UP_Z, DOWN_Z, SIBLING, OPPOSITE = range(6)
QKV_WINDOW = ((0, 0), (80, 10))
OUT_WINDOW = ((48, 6), (64, 8))


def normalise(values, shift, scale):
    mean = jnp.mean(values, axis=0, keepdims=True)
    centred = values - mean
    spread = jnp.mean(centred * centred, axis=0, keepdims=True)
    return (centred * lax.rsqrt(spread + 1e-06) * scale + shift).astype(jnp.bfloat16)


def kernel(
    x_ref, wqkv_ref, wout_ref, shift_ref, scale_ref, gate_ref, o_ref,
    slots, mod, qkv, heads, mixed, xt, nt, ft, sel_out, sel_in,
    tail, *rest_refs,
):
    bufs_a, bufs_b = rest_refs[:6], rest_refs[6:12]
    ring_send, ring_recv, a2a_send, a2a_recv, tail_sem, entered = rest_refs[12:]
    dp = lax.axis_index("dp")
    seq = lax.axis_index("seq")
    core, xlo = dp % 2, dp // 2
    hi, z, y = seq // 32, (seq // 4) % 8, seq % 4
    other = 1 - core

    def chip(yy, zz):
        return (dp, 32 * hi + 4 * ((zz + 8) % 8) + (yy + 4) % 4)

    sibling = (2 * xlo + other, seq)
    opposite = (2 * (1 - xlo) + core, 32 * (1 - hi) + 4 * z + y)
    beside = (2 * (1 - xlo) + core, seq)
    devices = (chip(y + 1, z), chip(y - 1, z), chip(y, z + 1), chip(y, z - 1), sibling, opposite)

    barrier = pltpu.get_barrier_semaphore()

    for device in (*devices, beside):
        pl.semaphore_signal(barrier, inc=1, device_id=device, device_id_type=MESH)

    columns = wqkv_ref[...].astype(jnp.float32)
    outs = wout_ref[...].astype(jnp.float32)
    rows = jnp.concatenate([columns[:, 0], outs[:, 0], outs[:, 1], columns[:, 1]], axis=0).astype(jnp.bfloat16)
    mine = 32 * hi + 4 * z + y
    slots[mine] = rows

    pl.semaphore_wait(barrier, 7)

    def part(slot, k):
        return slots.at[slot, pl.ds(PIECES[k][0], PIECES[k][1])]

    def push(slot, k, way):
        pltpu.make_async_remote_copy(
            src_ref=part(slot, k), dst_ref=part(slot, k),
            send_sem=ring_send.at[k, way], recv_sem=ring_recv.at[k, slot],
            device_id=devices[way], device_id_type=MESH,
        ).start()

    def arrive(slot, k):
        pltpu.make_async_remote_copy(
            src_ref=part(slot, k), dst_ref=part(slot, k),
            send_sem=ring_send.at[k, 0], recv_sem=ring_recv.at[k, slot],
            device_id=sibling, device_id_type=MESH,
        ).wait_recv()

    def routes(k, dy, dz):
        ways = []
        if PIECES[k][2] == "z":
            if dy == 0:
                ways += {0: [UP_Z, DOWN_Z], 3: [DOWN_Z] * (k % 2), 4: [], 5: [UP_Z] * (1 - k % 2)}.get(
                    dz, [DOWN_Z] if dz < 4 else [UP_Z]
                )
                ways += [UP_Y, DOWN_Y]
            elif dy != 2 and (dz + k) % 2 == dy // 2:
                ways += [DOWN_Y if dy == 1 else UP_Y]
        else:
            if dz == 0:
                ways += [UP_Z, DOWN_Z]
                if dy == 0:
                    ways += [UP_Y, DOWN_Y]
                elif dy != 2 and k % 2 == dy // 2:
                    ways += [DOWN_Y if dy == 1 else UP_Y]
            elif dz in (3, 5):
                if (dy + k) % 2 == dz // 4:
                    ways += [DOWN_Z if dz == 3 else UP_Z]
            elif dz != 4:
                ways += [DOWN_Z if dz < 4 else UP_Z]
        return ways

    def block_of(half, dy, dz):
        return 32 * half + 4 * lax.rem(z + dz, 8) + lax.rem(y + dy, 4)

    def event(k, dy, dz):
        slot = block_of(core, dy, dz)
        last = PIECES[k][3]
        start = dy == 0 and dz == 0

        def onward():
            for way in routes(k, dy, dz):
                push(slot, k, way)

        if start:

            @pl.when(hi != core)
            def _():
                arrive(slot, k)

            @pl.when(hi == core)
            def _():
                push(slot, k, OPPOSITE)
                if last:
                    onward()

            @pl.when(hi != core)
            def _():
                push(slot, k, SIBLING)

        else:
            arrive(slot, k)
            if last:

                @pl.when(hi == core)
                def _():
                    onward()
                    push(slot, k, OPPOSITE)

            push(slot, k, SIBLING)
        if not last:
            onward()

    def course(k):
        return [(k, dy, dz) for dy in range(4) for dz in range(8)]

    def run(events):
        for e in events:
            event(*e)

    def from_sibling(ks, dy, dz):
        slot = block_of(other, dy, dz)

        def taken():
            for k in ks:
                arrive(slot, k)

        if dy == 0 and dz == 0:
            pl.when(hi == core)(taken)
        else:
            taken()

    def all_from_sibling(ks):
        for dy in range(4):
            for dz in range(8):
                from_sibling(ks, dy, dz)

    order = [(e // 32, e // 8 % 4, e % 8) for e in ORDER]
    end_a = 1 + max(i for i, e in enumerate(order) if e[0] in GROUPS[0])
    run(order[:4])

    def prepare():
        six = jnp.concatenate([shift_ref[...], scale_ref[...], gate_ref[...], gate_ref[...]], axis=0)
        mod[...] = six.T
        xt[...] = x_ref[...].astype(jnp.float32).T
        nt[...] = normalise(xt[...], mod[:, 0:1], mod[:, 2:3])

    def token_at(by_frame, s, p):
        return 64 * p + s if by_frame else 4 * s + p

    def permutation(rows, cols):
        return jnp.where(rows == cols, 1.0, 0.0).astype(jnp.bfloat16)

    def make_sel_out(by_frame, q):
        row = lax.broadcasted_iota(jnp.int32, (256, 1), 0) + 256 * q
        want = 256 * ((row >> 2) & 3) + token_at(by_frame, row >> 4, row & 3)
        sel_out[by_frame, 256 * q : 256 * (q + 1)] = permutation(
            want, lax.broadcasted_iota(jnp.int32, (256, 1024), 1)
        )

    def make_sel_in(by_frame, q):
        col = lax.broadcasted_iota(jnp.int32, (1, 1024), 1)
        want = 256 * ((col >> 2) & 3) + token_at(by_frame, col >> 4, col & 3)
        sel_in[by_frame, 256 * q : 256 * (q + 1)] = permutation(
            lax.broadcasted_iota(jnp.int32, (256, 1024), 0) + 256 * q, want
        )

    def make_tail():
        row = lax.broadcasted_iota(jnp.int32, (256, 1), 0)
        col = lax.broadcasted_iota(jnp.int32, (1, 256), 1)
        rows = lax.broadcasted_iota(jnp.int32, (256, 256), 0)
        cols = lax.broadcasted_iota(jnp.int32, (256, 256), 1)
        for by_frame in (0, 1):
            tail[by_frame] = permutation(token_at(by_frame, row >> 2, row & 3), cols)
            sender = 4 * ((col >> 2) & 15) + (col >> 6)
            tail[2 + by_frame] = permutation(rows, token_at(by_frame, sender, col & 3))
        tail[4] = permutation(16 * ((row >> 2) & 15) + 4 * (row >> 6) + (row & 3), cols)

    def pack_and_send(bufs, by_frame, between=None):
        send_ref, recv_ref, line_out, line_in, _, _ = bufs
        line = seq // 4
        got = lax.dot_general(
            tail[by_frame], ft[1024:], (((1,), (1,)), ((), ())), preferred_element_type=jnp.float32
        )
        line_out[...] = got.astype(jnp.bfloat16).reshape(16, 16, 128)

        def along(k, _):
            to = lax.rem(line + k, 16)
            pltpu.make_async_remote_copy(
                src_ref=line_out.at[to], dst_ref=line_in.at[line],
                send_sem=tail_sem.at[0, by_frame], recv_sem=tail_sem.at[1, by_frame],
                device_id=(dp, 4 * to + y), device_id_type=MESH,
            ).start()
            return 0

        lax.fori_loop(1, 16, along, 0)
        line_in[line] = line_out[line]
        flat = jnp.concatenate([ft[256 * t : 256 * (t + 1)] for t in range(4)], axis=1)

        def quarter(c, _):
            q = lax.rem(seq // 16 + 1 + c, 4)
            packed = lax.dot_general(
                sel_out[by_frame, pl.ds(pl.multiple_of(256 * q, 256), 256)], flat,
                (((1,), (1,)), ((), ())), preferred_element_type=jnp.float32,
            )
            send_ref[pl.ds(16 * q, 16)] = packed.astype(jnp.bfloat16).reshape(16, 16, 256)

            def one(j, _):
                to = 16 * q + lax.rem(seq + j, 16)

                @pl.when(to != seq)
                def _():
                    pltpu.make_async_remote_copy(
                        src_ref=send_ref.at[to], dst_ref=recv_ref.at[seq],
                        send_sem=a2a_send.at[by_frame], recv_sem=a2a_recv.at[by_frame],
                        device_id=(dp, to), device_id_type=MESH,
                    ).start()

                return 0

            lax.fori_loop(0, 16, one, 0)
            return 0

        if between is None:
            lax.fori_loop(0, 4, quarter, 0)
        else:
            for c in range(4):
                between()
                quarter(c, 0)
        recv_ref[seq] = send_ref[seq]

    def relay(bufs, by_frame):
        _, _, line_out, line_in, y_out, y_in = bufs
        line = seq // 4
        finish(line_out.at[pl.ds(0, 15)], line_in.at[pl.ds(0, 15)], tail_sem.at[0, by_frame], tail_sem.at[1, by_frame])
        got = jnp.dot(tail[4], line_in[...].reshape(256, 128), preferred_element_type=jnp.float32)
        y_out[...] = got.astype(jnp.bfloat16).reshape(4, 64, 128)
        for k in range(1, 4):
            to = lax.rem(y + k, 4)
            pltpu.make_async_remote_copy(
                src_ref=y_out.at[to], dst_ref=y_in.at[y],
                send_sem=tail_sem.at[2, by_frame], recv_sem=tail_sem.at[3, by_frame],
                device_id=(dp, 4 * line + to), device_id_type=MESH,
            ).start()
        y_in[y] = y_out[y]

    def finish(src, dst, send, recv):
        done = pltpu.make_async_remote_copy(
            src_ref=src, dst_ref=dst, send_sem=send, recv_sem=recv, device_id=sibling, device_id_type=MESH
        )
        done.wait_send()
        done.wait_recv()

    def exchanged(bufs, by_frame):
        send_ref, recv_ref, _, _, y_out, y_in = bufs
        finish(y_out.at[pl.ds(0, 3)], y_in.at[pl.ds(0, 3)], tail_sem.at[2, by_frame], tail_sem.at[3, by_frame])
        finish(send_ref.at[pl.ds(0, 63)], recv_ref.at[pl.ds(0, 63)], a2a_send.at[by_frame], a2a_recv.at[by_frame])

    def unpack(bufs, by_frame):
        main = jnp.dot(
            sel_in[by_frame], bufs[1][...].reshape(1024, 256), preferred_element_type=jnp.float32
        )
        last = jnp.dot(tail[2 + by_frame], bufs[5][...].reshape(256, 128), preferred_element_type=jnp.float32)
        return [main[256 * t : 256 * (t + 1)] for t in range(4)] + [last]

    def project_slots(layer, slot_list):
        first = QKV_WINDOW[layer][0]
        block = jnp.concatenate([slots[j, pl.ds(first, 64)] for j in slot_list], axis=0)
        got = jnp.dot(block, nt[...], preferred_element_type=jnp.float32)
        for n, j in enumerate(slot_list):
            qkv[j] = got[64 * n : 64 * (n + 1)]

    def project_qkv(layer):
        def one(g, _):
            project_slots(layer, [8 * g + j for j in range(8)])
            return 0

        lax.fori_loop(0, 8, one, 0)

    def split_heads(layer, lo, hi_):
        offset = QKV_WINDOW[layer][1]

        def split(g, _):
            four = [qkv[4 * g + j, offset : offset + QKV_COLS] for j in range(4)]
            units = (
                jnp.concatenate([four[0], four[1][:18]], axis=0),
                jnp.concatenate([four[1][18:], four[2][:36]], axis=0),
                jnp.concatenate([four[2][36:], four[3]], axis=0),
            )
            for j, unit in enumerate(units):
                at = 3 * g + j
                factor = jnp.where(at < HEADS, HEAD_DIM**-0.5 * LOG2E, 1.0).astype(jnp.float32)
                heads[at] = (unit * factor).astype(jnp.bfloat16)
            return 0

        lax.fori_loop(lo, hi_, split, 0)

    def scores_of(h):
        return lax.dot_general(
            heads[HEADS + h], heads[h], (((0,), (0,)), ((), ())), preferred_element_type=jnp.float32
        )

    def mix(h, weights, total):
        got = jnp.dot(heads[2 * HEADS + h], weights, preferred_element_type=jnp.float32)
        mixed[pl.ds(pl.multiple_of(HEAD_DIM * h, 8), HEAD_DIM)] = got / total

    def attend_space(h):
        scores = scores_of(h)
        weights = jnp.exp2(scores - jnp.max(scores, axis=0, keepdims=True))
        total = jnp.sum(weights, axis=0, keepdims=True)
        mix(h, weights.astype(jnp.bfloat16), total)

    def attend_time(h):
        scores = scores_of(h)
        low = lax.broadcasted_iota(jnp.int32, (64, 128), 1) < 64
        near = jnp.concatenate(
            [
                jnp.where(low, scores[0:64, 0:128], scores[64:128, 0:128]),
                jnp.where(low, scores[128:192, 128:256], scores[192:256, 128:256]),
            ],
            axis=1,
        )
        weights = jnp.exp2(near - jnp.max(near, axis=0, keepdims=True))
        total = jnp.sum(weights, axis=0, keepdims=True)
        column = lax.broadcasted_iota(jnp.int32, (64, TOKENS), 1) // 64
        spread = jnp.concatenate([jnp.where(column == p, weights, 0.0) for p in range(4)], axis=0)
        mix(h, spread.astype(jnp.bfloat16), total)

    def project_out(layer, lo, hi_):
        first, offset = OUT_WINDOW[layer]

        def one(g, _):
            block = slots[pl.ds(8 * g, 8), pl.ds(first, 32)].reshape(256, WIDTH)
            got = jnp.dot(block, nt[...], preferred_element_type=jnp.float32).reshape(8, 32, TOKENS)
            got = jnp.concatenate([got[j, offset : offset + OUT_COLS] for j in range(8)], axis=0)
            at = pl.ds(pl.multiple_of(144 * g, 16), 144)
            ft[at] = (xt[at] + mod[at, 4 + layer : 5 + layer] * got).astype(jnp.bfloat16)
            return 0

        lax.fori_loop(lo, hi_, one, 0)

    def over_heads(attend, lo, hi_, step=2):
        def one(n, _):
            for j in range(step):
                attend(lo + step * n + j)
            return 0

        lax.fori_loop(0, (hi_ - lo) // step, one, 0)

    done = {}
    for i, (k, dy, dz) in enumerate(order[:end_a]):
        if k in GROUPS[0]:
            done[dy, dz] = i
    blocks = sorted(done, key=done.get)
    batches = [blocks[n : n + 4] for n in range(0, 32, 4)]
    after = {}
    tasks = [make_tail]
    for by_frame in (0, 1):
        tasks += [functools.partial(make_sel_out, by_frame, q) for q in range(4)]
    tasks += [functools.partial(make_sel_in, 0, q) for q in range(4)]
    for n, task in enumerate([prepare] + tasks):
        after.setdefault(6 + 4 * n, []).append(task)

    def batch(n):
        ready = [block_of(core, dy, dz) for dy, dz in batches[n]] if n < 8 else []
        if n > 0:
            for dy, dz in batches[n - 1]:
                from_sibling(GROUPS[0], dy, dz)
                ready.append(block_of(other, dy, dz))
        project_slots(0, ready)

    for n in range(8):
        after.setdefault(max(done[block] for block in batches[n]), []).append(functools.partial(batch, n))
    for i in range(4, end_a):
        run(order[i : i + 1])
        for task in after.get(i, []):
            task()
    batch(8)

    def tell(n, device):
        pl.semaphore_signal(entered.at[n], inc=1, device_id=device, device_id_type=MESH)

    tell(0, opposite)

    rest = order[end_a:]

    def more(count):
        run(rest[:count])
        del rest[:count]

    for q in range(4):
        split_heads(0, 4 * q, 4 * q + 4)
        more(2)
    for q in range(8):
        over_heads(attend_space, 2 * q, 2 * q + 2)
        more(2)
    pl.semaphore_wait(entered.at[0], 1)
    tell(1, beside)
    if GROUPS[1]:
        more(1 + max([i for i, e in enumerate(rest) if e[0] in GROUPS[1]], default=-1))
        all_from_sibling(GROUPS[1])
    nt[...] = mixed[...].astype(jnp.bfloat16)
    for q in range(4):
        project_out(0, 2 * q, 2 * q + 2)
        more(2)
    pl.semaphore_wait(entered.at[1], 1)
    pack_and_send(bufs_a, 0, functools.partial(more, 4))
    more(len(rest) // 2)
    relay(bufs_a, 0)
    more(len(rest))
    all_from_sibling(GROUPS[2])
    exchanged(bufs_a, 0)

    got = lax.dot_general(
        bufs_a[1][...].reshape(1024, 256), sel_out[1],
        (((0,), (0,)), ((), ())), preferred_element_type=jnp.float32,
    )
    for t in range(4):
        xt[256 * t : 256 * (t + 1)] = got[:, 256 * t : 256 * (t + 1)]
    last = jnp.dot(tail[3], bufs_a[5][...].reshape(256, 128), preferred_element_type=jnp.float32)
    xt[1024:] = last.T
    nt[...] = normalise(xt[...], mod[:, 1:2], mod[:, 3:4])
    project_qkv(1)
    split_heads(1, 0, 16)
    over_heads(attend_time, 0, HEADS, 4)
    nt[...] = mixed[...].astype(jnp.bfloat16)
    project_out(1, 0, 8)
    pack_and_send(bufs_b, 1)
    relay(bufs_b, 1)
    exchanged(bufs_b, 1)
    for t, got in enumerate(unpack(bufs_b, 0)):
        o_ref[:, 256 * t : 256 * t + got.shape[1]] = got.astype(jnp.bfloat16)

    def sent(k, way, count):
        rows = pl.ds(PIECES[k][0], PIECES[k][1])
        pltpu.make_async_remote_copy(
            src_ref=slots.at[pl.ds(0, count), rows], dst_ref=slots.at[pl.ds(0, count), rows],
            send_sem=ring_send.at[k, way], recv_sem=ring_recv.at[k, 0],
            device_id=sibling, device_id_type=MESH,
        ).wait_send()

    for k, piece in enumerate(PIECES):
        ways = [way for e in course(k) for way in routes(*e)]

        def plane_sent():
            for way in (UP_Y, DOWN_Y, UP_Z, DOWN_Z):
                sent(k, way, ways.count(way))

        if not piece[3]:
            plane_sent()

        @pl.when(hi == core)
        def _():
            if piece[3]:
                plane_sent()
            sent(k, OPPOSITE, 32 if piece[3] else 1)
            sent(k, SIBLING, 31)

        @pl.when(hi != core)
        def _():
            sent(k, SIBLING, 32)


def per_device(tokens, w_qkv, w_out, mod_shift, mod_scale, mod_gate):
    vmem = pl.BlockSpec(memory_space=pltpu.VMEM)
    exchange_buffers = [
        pltpu.VMEM(shape, jnp.bfloat16)
        for shape in ((64, 16, 256), (64, 16, 256), (16, 16, 128), (16, 16, 128), (4, 64, 128), (4, 64, 128))
    ]
    result = pl.pallas_call(
        kernel,
        out_shape=jax.ShapeDtypeStruct((TOKENS, WIDTH), jnp.bfloat16),
        in_specs=[vmem] * 6,
        out_specs=vmem,
        scratch_shapes=[
            pltpu.VMEM((64, SLOT_ROWS, WIDTH), jnp.bfloat16),
            pltpu.VMEM((WIDTH, 8), jnp.float32),
            pltpu.VMEM((64, 64, TOKENS), jnp.float32),
            pltpu.VMEM((3 * HEADS, HEAD_DIM, TOKENS), jnp.bfloat16),
            pltpu.VMEM((WIDTH, TOKENS), jnp.float32),
            pltpu.VMEM((WIDTH, TOKENS), jnp.float32),
            pltpu.VMEM((WIDTH, TOKENS), jnp.bfloat16),
            pltpu.VMEM((WIDTH, TOKENS), jnp.bfloat16),
            pltpu.VMEM((2, 1024, 1024), jnp.bfloat16),
            pltpu.VMEM((1, 1024, 1024), jnp.bfloat16),
            pltpu.VMEM((5, 256, 256), jnp.bfloat16),
            *exchange_buffers,
            *exchange_buffers,
            pltpu.SemaphoreType.DMA((len(PIECES), 6)),
            pltpu.SemaphoreType.DMA((len(PIECES), 64)),
            pltpu.SemaphoreType.DMA((2,)),
            pltpu.SemaphoreType.DMA((2,)),
            pltpu.SemaphoreType.DMA((4, 2)),
            pltpu.SemaphoreType.REGULAR((2,)),
        ],
        compiler_params=pltpu.CompilerParams(
            collective_id=0, has_side_effects=True, vmem_limit_bytes=60 * 2**20
        ),
        name="latte",
    )(
        tokens.reshape(TOKENS, WIDTH),
        jnp.transpose(w_qkv, (2, 0, 1)),
        jnp.transpose(w_out, (2, 0, 1)),
        mod_shift,
        mod_scale,
        mod_gate,
    )
    return result.reshape(tokens.shape)


def solution(mesh):
    in_specs = (
        P("dp", "seq", None, None),
        P(None, None, "seq"),
        P(None, None, "seq"),
        P(),
        P(),
        P(),
    )
    return jax.shard_map(
        per_device, mesh=mesh, in_specs=in_specs, out_specs=P("dp", "seq", None, None), check_vma=False
    )
```
